256 devices in a mesh: dp: 16 (over y, x), token: 16 (over z, core).
Axes of the slice: x: 4, y: 4, z: 8, core: 2. Of those that a mesh axis runs over, the one named last changes fastest.
Arguments:
- mix_input: bfloat16 [6144, 16, 768], P('dp', 'token'), may hold values from -6 to 6
- out_grad: bfloat16 [6144, 16, 768], P('dp', 'token'), may hold values from -1.5 to 1.5
- w_up: bfloat16 [16, 768, 3072], P('token'), may hold values from -0.21875 to 0.21875
- w_down: bfloat16 [16, 3072, 768], P('token'), may hold values from -0.109375 to 0.109375
- gain_first: float32 [16, 768], P('token'), may hold values from 0.25 to 1.75
- gain_second: float32 [16, 768], P('token'), may hold values from 0.25 to 1.75
- owner_dev: int32 [16, 6144, 1], P('token', 'dp'), may hold values from 0 to 15; in each aligned block of 384 rows (0 to 383, 384 to 767, ..., all dimensions but the last counted through in order) at most 56 rows name the same one
- slot_row: int32 [16, 6144], P('token', 'dp'), may hold values from 0 to 255
Outputs:
- grad_up: float32 [16, 768, 3072], P('token', 'dp')
- grad_down: float32 [16, 3072, 768], P('token', 'dp')
- row_grad: float32 [16, 4096, 768], P('token', 'dp')
The draws below stay inside these ranges and needn't reach their ends.
Inputs may be any that keep to these rules, and one draw needn't show every extreme that they name: `owner_dev`: in the rows of one device (aligned blocks of 384 samples of one token) no owner is named by more than 56 rows, a bound that some block reaches.
All inputs are finite; a program needn't handle non-finite values.
Results may differ from the reference program's by a relative error of at most 0.015.
Values may be sent and summed in bfloat16 or wider, within the bound.
No kernel may reach another device: no remote copies, remote signals or barrier semaphores. Data moves between devices by JAX's collectives and lax.ppermute only.
A program may use at most 128 MiB of HBM per device.

```python
import math
import jax
import jax.numpy as jnp
import numpy as np
from jax import lax

D = 768
F = 3072
B_DEV = 384
HOT = 256
NTOK = 16
HS = 48
BATCH = 6144
CAP = 56
N_DP = 16


def touch_ends(result, own_key, smallest, top_value):
    longest = result.shape.index(max(result.shape))
    spots = []
    for shift in (0, 1):
        where = [jax.random.randint(jax.random.fold_in(own_key, axis), (), 0, length) for axis, length in enumerate(result.shape)]
        where[longest] = (where[longest] + shift) % result.shape[longest]
        spots.append(tuple(where))
    return result.at[spots[0]].set(smallest).at[spots[1]].set(top_value)


def shard_levels(own_key, dims, shards, low, largest):
    factor_of, own = 1.0, jax.random.fold_in(own_key, 6)
    for dim, blocks in shards:
        steps = jnp.exp(jax.random.uniform(jax.random.fold_in(own, dim), (blocks,), jnp.float32, low / len(shards), largest / len(shards)))
        factor_of = factor_of * jnp.repeat(steps, dims[dim] // blocks).reshape([-1 if axis == dim else 1 for axis in range(len(dims))])
    return factor_of


def rank_table(amount, slope):
    weights = [(1 << 20) // math.isqrt(rank ** slope) + 1 for rank in range(1, amount + 1)]
    spread = 1 + sum(weights) // (1 << 30)
    return np.cumsum(np.array([max(1, weight // spread) for weight in weights]))


def ranked_ids(own_key, dims, number_of, slope):
    grid = rank_table(number_of, slope)
    ticket = jax.random.randint(jax.random.fold_in(own_key, 1), dims, 0, int(grid[number_of - 1]))
    grade = jnp.searchsorted(jnp.asarray(grid, jnp.int32), ticket, side="right")
    return jax.random.permutation(jax.random.fold_in(own_key, 2), number_of)[grade].astype(jnp.int32)


def shared_out(stream_key, own, number, rows, number_of, top, limit, lean):
    sequence = jax.random.permutation(stream_key, number_of)
    crowded, ordinary = portions_of(number_of, rows * top, limit, lean, True), portions_of(number_of, rows * top, limit, lean, False)
    places = jnp.arange(number_of)

    def named(tallies, turn):
        used = int((tallies > 0).sum())
        fixed = max(1, used // 4)
        shifted = fixed + (places - fixed + turn * (used - fixed)) % max(1, number_of - fixed)
        return jnp.zeros((number_of,), jnp.int32).at[sequence[jnp.where(places < fixed, places, shifted)]].set(jnp.asarray(tallies, jnp.int32))

    tallies = jnp.where(number % 4 == 0, named(crowded, number // 4), named(ordinary, number - number // 4 - 1))
    mixed = jax.random.permutation(jax.random.fold_in(own, 3), number_of)
    donor, sink = mixed[0:number_of // 2 * 2:2], mixed[1:number_of // 2 * 2:2]
    margin = jnp.minimum(tallies[donor] - 1, limit - tallies[sink]) // 2
    margin = jnp.where((donor == sequence[0]) | (sink == sequence[0]) | (tallies[sink] == 0), 0, jnp.maximum(margin, 0))
    shifted = jax.random.randint(jax.random.fold_in(own, 4), (number_of // 2,), 0, 1 << 20) % (margin + 1)
    tallies = tallies.at[donor].add(-shifted).at[sink].add(shifted)
    labels = jnp.searchsorted(jnp.cumsum(tallies), jnp.arange(rows * top), side="right").astype(jnp.int32)
    grid = labels.reshape(top, rows).T
    grid = grid[jax.random.permutation(jax.random.fold_in(own, 1), rows)]
    turn = jax.random.randint(jax.random.fold_in(own, 2), (rows, 1), 0, top)
    return jnp.take_along_axis(grid, (jnp.arange(top)[None, :] + turn) % top, axis=1)


def portions_of(count, total, limit, slope, full):
    portions = [(1 << 20) // math.isqrt(standing ** slope) + 1 for standing in range(1, count + 1)]
    largest = limit if full else min(limit, max(-(-total // count), total * portions[0] // sum(portions)))
    least = 1 if total - largest >= count - 1 else 0
    counts, rest = [largest] + [least] * (count - 1), total - largest - least * (count - 1)
    while rest > 0:
        candidates = [i for i in range(1, count) if counts[i] < largest] or [i for i in range(1, count) if counts[i] < limit]
        pool, remaining = sum([portions[i] for i in candidates]), rest
        for i in candidates:
            addition = min(limit - counts[i], max(1, remaining * portions[i] // pool), rest)
            counts[i] = counts[i] + addition
            rest = rest - addition
    return np.array(counts)


def centred(key, extent, deviation, limit, split=(), dtype=jnp.bfloat16):
    entries = jax.random.normal(key, extent, jnp.float32) * deviation
    if len(split) > 0:
        entries = shard_levels(key, extent, split, -0.22, 0.18) * entries
    return jnp.clip(entries, min=-limit, max=limit).astype(dtype)


def setup_inputs(seed: int = 0) -> dict:
    streams_of = jax.random.split(jax.random.key(seed), 9)
    mix_input = centred(streams_of[0], (BATCH, NTOK, D), 1.0, 6.0, ((0, 16), (1, 16)))
    out_grad = centred(streams_of[1], (BATCH, NTOK, D), 0.25, 1.5, ((0, 16), (1, 16)))
    w_up = centred(streams_of[2], (NTOK, D, F), D ** -0.5, 0.21875, ((0, 16),))
    w_down = centred(streams_of[3], (NTOK, F, D), F ** -0.5, 0.109375, ((0, 16),))
    gain_first = jnp.clip(1.0 + 0.15 * jax.random.normal(streams_of[4], (NTOK, D), jnp.float32), 0.25, 1.75)
    gain_second = jnp.clip(1.0 + 0.15 * jax.random.normal(streams_of[5], (NTOK, D), jnp.float32), 0.25, 1.75)
    owner_dev_keys = jax.random.split(jax.random.fold_in(streams_of[6], 1), NTOK * BATCH // B_DEV)
    owner_dev_turns = jax.random.permutation(jax.random.fold_in(streams_of[6], 3), NTOK * BATCH // B_DEV)
    owner_dev = jax.vmap(lambda own, number: shared_out(jax.random.fold_in(streams_of[6], 2), own, number, B_DEV, N_DP, 1, CAP, 2))(owner_dev_keys, owner_dev_turns).reshape((NTOK, BATCH, 1))
    slot_row = touch_ends(ranked_ids(streams_of[7], (NTOK, BATCH), HOT, 2), jax.random.fold_in(streams_of[7], 3), 0, HOT - 1).astype(jnp.int32)
    return dict(mix_input=mix_input, out_grad=out_grad, w_up=w_up, w_down=w_down, gain_first=gain_first, gain_second=gain_second, owner_dev=owner_dev, slot_row=slot_row)


EPS = 1e-05
HALF_ROOT = 0.7071067811865476
INV_ROOT_TAU = 0.3989422804014327

def normalize(values):
    center = values - lax.optimization_barrier(jnp.mean(values, axis=-1, keepdims=True))
    inv_scale = lax.rsqrt(lax.optimization_barrier(jnp.mean(center * center, axis=-1, keepdims=True)) + EPS)
    return (center * inv_scale, inv_scale)

def norm_back(grad_norm, normed, inv_scale):
    mean_grad = lax.optimization_barrier(jnp.mean(grad_norm, axis=-1, keepdims=True))
    mean_proj = lax.optimization_barrier(jnp.mean(grad_norm * normed, axis=-1, keepdims=True))
    return inv_scale * (grad_norm - mean_grad - normed * mean_proj)

def gelu_parts(pre_act):
    cumul = 0.5 * (1.0 + jax.scipy.special.erf(pre_act * HALF_ROOT))
    density = jnp.exp(-0.5 * pre_act * pre_act) * INV_ROOT_TAU
    return (pre_act * cumul, cumul + pre_act * density)

def group_partial(left, right):
    left_parts = left.reshape(N_DP, B_DEV, left.shape[1]).astype(jnp.float32)
    right_parts = right.reshape(N_DP, B_DEV, right.shape[1]).astype(jnp.float32)
    partial_sums = jnp.einsum('nba,nbc->nac', left_parts, right_parts).astype(jnp.bfloat16)
    partial_sums = lax.optimization_barrier(partial_sums)
    return lax.optimization_barrier(jnp.sum(partial_sums.astype(jnp.float32), axis=0))

def per_token(inputs):
    mix_slab, grad_slab, up_mat, down_mat, gain_one, gain_two = inputs
    normed, inv_scale = normalize(mix_slab.astype(jnp.float32))
    hidden_in = (normed * gain_one).astype(jnp.bfloat16)
    pre_act = jnp.dot(hidden_in, up_mat, preferred_element_type=jnp.float32)
    act_value, act_slope = gelu_parts(pre_act)
    active = act_value.astype(jnp.bfloat16)
    outer_sum = jnp.dot(active, down_mat, preferred_element_type=jnp.float32) + hidden_in.astype(jnp.float32)
    normed_out, inv_out = normalize(outer_sum)
    grad_wide = norm_back(grad_slab.astype(jnp.float32) * gain_two, normed_out, inv_out)
    grad_mid = grad_wide.astype(jnp.bfloat16)
    grad_act = jnp.dot(grad_mid, down_mat.T, preferred_element_type=jnp.float32)
    grad_pre = (grad_act * act_slope).astype(jnp.bfloat16)
    grad_up = group_partial(hidden_in, grad_pre)
    grad_down = group_partial(active, grad_mid)
    grad_hidden = jnp.dot(grad_pre, up_mat.T, preferred_element_type=jnp.float32) + grad_wide
    grad_sum = norm_back(grad_hidden * gain_one, normed, inv_scale).astype(jnp.bfloat16)
    return (grad_up, grad_down, grad_sum)

def reference(mix_input, out_grad, w_up, w_down, gain_first, gain_second, owner_dev, slot_row):
    mix_tok = jnp.swapaxes(mix_input, 0, 1)
    grad_tok = jnp.swapaxes(out_grad, 0, 1)
    grad_up, grad_down, grad_sum = lax.map(per_token, (mix_tok, grad_tok, w_up, w_down, gain_first, gain_second))
    pieces = grad_sum.reshape(NTOK, BATCH, NTOK, HS)
    swapped = jnp.transpose(pieces, (2, 1, 0, 3)).reshape(NTOK, BATCH, D)
    embed_grad = (grad_sum.astype(jnp.float32) + swapped.astype(jnp.float32)).astype(jnp.bfloat16)
    target = owner_dev[:, :, 0] * HOT + slot_row

    def table_sum(grad_rows, target_rows):
        return jax.ops.segment_sum(grad_rows.astype(jnp.float32), target_rows, num_segments=N_DP * HOT)
    row_grad = jax.vmap(table_sum)(embed_grad, target)
    return (grad_up, grad_down, row_grad)
```

```python
import jax
import jax.numpy as jnp
from jax import lax
from jax.sharding import PartitionSpec as P

HOT = 256
CAP = 56
SEAT = 64


EPS = 1e-05
HALF_ROOT = 0.7071067811865476
INV_ROOT_TAU = 0.3989422804014327


def normalize(values):
    center = values - jnp.mean(values, axis=-1, keepdims=True)
    inv_scale = lax.rsqrt(jnp.mean(center * center, axis=-1, keepdims=True) + EPS)
    return (center * inv_scale, inv_scale)


def norm_back(grad_norm, normed, inv_scale):
    mean_grad = jnp.mean(grad_norm, axis=-1, keepdims=True)
    mean_proj = jnp.mean(grad_norm * normed, axis=-1, keepdims=True)
    return inv_scale * (grad_norm - mean_grad - normed * mean_proj)


def gelu_parts(pre_act):
    cumul = 0.5 * (1.0 + jax.scipy.special.erf(pre_act * HALF_ROOT))
    density = jnp.exp(-0.5 * pre_act * pre_act) * INV_ROOT_TAU
    return (pre_act * cumul, cumul + pre_act * density)


def contract_rows(left, right):
    return lax.dot_general(
        left, right, (((0,), (0,)), ((), ())), preferred_element_type=jnp.float32
    )


def contract_cols(left, right):
    return lax.dot_general(
        left, right, (((1,), (1,)), ((), ())), preferred_element_type=jnp.float32
    )


def per_device(mix_input, out_grad, w_up, w_down, gain_first, gain_second, owner_dev, slot_row):
    batch_rows = mix_input.shape[0]
    width = mix_input.shape[2]
    owners = lax.axis_size("dp")
    normed, inv_scale = normalize(mix_input[:, 0, :].astype(jnp.float32))
    hidden_in = (normed * gain_first[0]).astype(jnp.bfloat16)
    pre_act = jnp.dot(hidden_in, w_up[0], preferred_element_type=jnp.float32)
    act_value, act_slope = gelu_parts(pre_act)
    active = act_value.astype(jnp.bfloat16)
    outer_sum = jnp.dot(active, w_down[0], preferred_element_type=jnp.float32) + hidden_in.astype(
        jnp.float32
    )
    normed_out, inv_out = normalize(outer_sum)
    grad_wide = norm_back(
        out_grad[:, 0, :].astype(jnp.float32) * gain_second[0], normed_out, inv_out
    )
    grad_mid = grad_wide.astype(jnp.bfloat16)
    grad_act = contract_cols(grad_mid, w_down[0])
    grad_pre = (grad_act * act_slope).astype(jnp.bfloat16)
    up_whole = contract_rows(hidden_in, grad_pre).astype(jnp.bfloat16)
    down_whole = contract_rows(active, grad_mid).astype(jnp.bfloat16)
    up_rows, down_rows = width // owners, down_whole.shape[0] // owners
    both = jnp.concatenate(
        [up_whole.reshape(owners, -1, width), down_whole.reshape(owners, -1, width)], axis=1
    )
    both = lax.psum_scatter(both, "dp", scatter_dimension=0, tiled=False).astype(jnp.float32)
    grad_up = both[: both.shape[0] // 2].reshape(up_rows, -1)
    grad_down = both[both.shape[0] // 2 :].reshape(down_rows, width)
    grad_hidden = contract_cols(grad_pre, w_up[0]) + grad_wide
    grad_sum = norm_back(grad_hidden * gain_first[0], normed, inv_scale).astype(jnp.bfloat16)
    pieces = lax.axis_size("token")
    swapped = lax.all_to_all(
        grad_sum.reshape(batch_rows, pieces, width // pieces),
        "token",
        split_axis=1,
        concat_axis=1,
        tiled=True,
    )
    embed_grad = (
        grad_sum.astype(jnp.float32) + swapped.reshape(batch_rows, width).astype(jnp.float32)
    ).astype(jnp.bfloat16)
    owner_hot = (
        lax.broadcasted_iota(jnp.int32, (owners, batch_rows), 0) == owner_dev[0, :, 0][None, :]
    )
    earlier = (
        lax.broadcasted_iota(jnp.int32, (batch_rows, batch_rows), 0)
        < lax.broadcasted_iota(jnp.int32, (batch_rows, batch_rows), 1)
    ).astype(jnp.bfloat16)
    ahead = jnp.dot(owner_hot.astype(jnp.bfloat16), earlier, preferred_element_type=jnp.float32)
    rank = jnp.sum(jnp.where(owner_hot, ahead, 0.0), axis=0).astype(jnp.int32)
    rank_hot = lax.broadcasted_iota(jnp.int32, (SEAT, batch_rows), 0) == rank[None, :]
    slot_next = jnp.where(owner_hot, slot_row + 1, 0).astype(jnp.bfloat16)
    slots = contract_cols(slot_next, rank_hot.astype(jnp.bfloat16))
    seat = owner_dev[0, :, 0] * SEAT + rank
    picker = (
        lax.broadcasted_iota(jnp.int32, (owners * SEAT, batch_rows), 0) == seat[None, :]
    ).astype(jnp.bfloat16)
    sent = jnp.dot(picker, embed_grad, preferred_element_type=jnp.float32).astype(jnp.bfloat16)
    sent = jnp.concatenate(
        [
            sent.reshape(owners, SEAT, width)[:, :CAP],
            jnp.pad(slots.astype(jnp.bfloat16), ((0, 0), (0, width - SEAT)))[:, None, :],
            jnp.zeros((owners, SEAT - CAP - 1, width), jnp.bfloat16),
        ],
        axis=1,
    )
    landed = lax.all_to_all(sent, "dp", split_axis=0, concat_axis=0, tiled=True)
    slots_in = landed[:, CAP, :SEAT].astype(jnp.int32) - 1
    placer = (
        lax.broadcasted_iota(jnp.int32, (HOT, owners, SEAT), 0) == slots_in[None]
    ).astype(jnp.bfloat16)
    row_grad = jnp.dot(
        placer.reshape(HOT, owners * SEAT),
        landed.reshape(owners * SEAT, width),
        preferred_element_type=jnp.float32,
    )
    return (grad_up[None], grad_down[None], row_grad[None])


def solution(mesh):
    placed = (
        P("dp", "token", None),
        P("dp", "token", None),
        P("token", None, None),
        P("token", None, None),
        P("token", None),
        P("token", None),
        P("token", "dp", None),
        P("token", "dp"),
    )
    return jax.shard_map(
        per_device,
        mesh=mesh,
        in_specs=placed,
        out_specs=(P("token", "dp", None), P("token", "dp", None), P("token", "dp", None)),
        check_vma=False,
    )
```

```python
import functools

import jax
import jax.numpy as jnp
from jax import lax
from jax.experimental import pallas as pl
from jax.experimental.pallas import tpu as pltpu
from jax.sharding import PartitionSpec as P

HOT = 256
CAP = 56
SEAT = 64
SIDE = 4
BLOCK = 48
ROWS = 16

EPS = 1e-05
HALF_ROOT = 0.7071067811865476
INV_ROOT_TAU = 0.3989422804014327
F32 = jnp.float32
BF16 = jnp.bfloat16

ROLE = ((6, 4, 0, 3), (7, 1, 2, 5))


def normalize(values):
    center = values - jnp.mean(values, axis=-1, keepdims=True)
    inv_scale = lax.rsqrt(jnp.mean(center * center, axis=-1, keepdims=True) + EPS)
    return (center * inv_scale, inv_scale)


def norm_back(grad_norm, normed, inv_scale):
    mean_grad = jnp.mean(grad_norm, axis=-1, keepdims=True)
    mean_proj = jnp.mean(grad_norm * normed, axis=-1, keepdims=True)
    return inv_scale * (grad_norm - mean_grad - normed * mean_proj)


def gelu_parts(pre_act):
    cumul = 0.5 * (1.0 + lax.erf(pre_act * HALF_ROOT))
    density = jnp.exp(-0.5 * pre_act * pre_act) * INV_ROOT_TAU
    return (pre_act * cumul, cumul + pre_act * density)


def contract_rows(left, right):
    return lax.dot_general(left, right, (((0,), (0,)), ((), ())), preferred_element_type=F32)


def contract_cols(left, right):
    return lax.dot_general(left, right, (((1,), (1,)), ((), ())), preferred_element_type=F32)


def send_out(stage, outs, sems):
    copies = [
        pltpu.make_async_copy(stage.at[pl.ds(8 * k, 8)], out, sems.at[k])
        for k, out in enumerate(outs)
    ]
    for copy in copies:
        copy.start()
    for copy in copies:
        copy.wait()


def forward_kernel(dest, mix, out_grad, w_up, w_down, gain_first, gain_second, *refs):
    hidden, slope, grad_wide, grad_mid = refs[:4]
    outs, (active, stage, sems) = refs[4:12], refs[12:]
    step = pl.program_id(0)

    @pl.when(step == 0)
    def _():
        normed, _ = normalize(mix[...].astype(F32))
        hidden[...] = (normed * gain_first[...]).astype(BF16)

    @pl.when(step < SIDE)
    def _():
        pre_act = jnp.dot(hidden[...], w_up[...], preferred_element_type=F32)
        act_value, act_slope = gelu_parts(pre_act)
        act_value = act_value.astype(BF16)
        active[step] = act_value
        slope[0] = act_slope
        part = jnp.dot(act_value, w_down[...], preferred_element_type=F32)

        @pl.when(step == 0)
        def _():
            grad_wide[...] = part + hidden[...].astype(F32)

        @pl.when(step > 0)
        def _():
            grad_wide[...] += part

    @pl.when(step == SIDE - 1)
    def _():
        normed_out, inv_out = normalize(grad_wide[...])
        wide = norm_back(out_grad[...].astype(F32) * gain_second[...], normed_out, inv_out)
        grad_wide[...] = wide
        grad_mid[...] = wide.astype(BF16)

    @pl.when(step >= SIDE)
    def _():
        part = contract_rows(active[step - SIDE], grad_mid[...]).astype(BF16)
        for k in range(16):
            stage[dest[(step - SIDE) * 16 + k]] = part[k * BLOCK : (k + 1) * BLOCK]

    @pl.when(step == 2 * SIDE - 1)
    def _():
        send_out(stage, outs, sems)


def backward_kernel(
    dest, mix, hidden, slope, grad_wide, grad_mid, w_up, w_down, gain_first, *refs
):
    grad_sum, outs = refs[0], refs[1:9]
    turned, grad_hidden, stage, sems = refs[9:]
    step = pl.program_id(0)

    @pl.when(step == 0)
    def _():
        turned[...] = hidden[...].T

    grad_act = contract_cols(grad_mid[...], w_down[...])
    grad_pre = (grad_act * slope[0]).astype(BF16)
    part = jnp.dot(turned[...], grad_pre, preferred_element_type=F32).astype(BF16)
    for k in range(16):
        stage[dest[k * 4 + step]] = part[k * BLOCK : (k + 1) * BLOCK]
    part = contract_cols(grad_pre, w_up[...])

    @pl.when(step == 0)
    def _():
        grad_hidden[...] = part + grad_wide[...]

    @pl.when(step > 0)
    def _():
        grad_hidden[...] += part

    @pl.when(step == SIDE - 1)
    def _():
        normed, inv_scale = normalize(mix[...].astype(F32))
        total = norm_back(grad_hidden[...] * gain_first[...], normed, inv_scale)
        grad_sum[...] = total.T.astype(BF16)
        send_out(stage, outs, sems)


def seat_kernel(grad_sum, swapped, owner, slot, sent):
    owners, rows = sent.shape[0], owner.shape[1]
    width = sent.shape[2]
    iota = functools.partial(lax.broadcasted_iota, jnp.int32)
    embed = (grad_sum[...].astype(F32) + swapped[...].astype(F32)).astype(BF16)
    owner_hot = iota((owners, rows), 0) == owner[...]
    earlier = (iota((rows, rows), 0) < iota((rows, rows), 1)).astype(F32).astype(BF16)
    ahead = jnp.dot(
        owner_hot.astype(F32).astype(BF16), earlier, preferred_element_type=F32
    )
    rank = jnp.sum(jnp.where(owner_hot, ahead, 0.0), axis=0, keepdims=True).astype(jnp.int32)
    rank_hot = (iota((width, rows), 0) == rank).astype(F32).astype(BF16)
    slot_next = jnp.where(owner_hot, (slot[...] + 1).astype(F32), 0.0).astype(BF16)
    slots = contract_cols(slot_next, rank_hot)
    seat = owner[...] * SEAT + rank
    picker = (iota((owners * SEAT, rows), 0) == seat).astype(F32).astype(BF16)
    chosen = contract_cols(picker, embed).reshape(owners, SEAT, width)
    at_cap = iota((1, SEAT, 1), 1) == CAP
    sent[...] = jnp.where(at_cap, slots[:, None, :], chosen).astype(BF16)


def add(*refs):
    total = refs[0].astype(F32)
    for ref in refs[1:]:
        total = total + ref.astype(F32)
    return total


def first_kernel(*refs):
    ins, outs = refs[:-4], refs[-4:]
    for axis in range(2):
        for mat in range(2):
            keep, up, down = ins[(axis * 2 + mat) * 3 : (axis * 2 + mat) * 3 + 3]
            rows = pl.ds(mat * SIDE, SIDE)
            outs[axis * 2][rows] = add(keep[:SIDE], up[...]).astype(BF16)
            outs[axis * 2 + 1][rows] = add(keep[SIDE:], down[...]).astype(BF16)


def second_kernel(*refs):
    ins, outs = refs[:-8], refs[-8:]
    for axis in range(2):
        up2, down2, mid2, keep2 = outs[axis * 4 : axis * 4 + 4]
        here = ins[axis * 8 : axis * 8 + 8]
        for mat in range(2):
            keep, up, down = here[mat * 3 : mat * 3 + 3]
            rows = slice(mat * SIDE, (mat + 1) * SIDE)
            low = add(keep[:SIDE], down[...], here[6][rows])
            high = add(keep[SIDE:], up[...], here[7][rows])
            up2[2 * mat] = low[2].astype(BF16)
            up2[2 * mat + 1] = high[1].astype(BF16)
            down2[2 * mat] = high[2].astype(BF16)
            down2[2 * mat + 1] = low[3].astype(BF16)
            mid2[2 * mat] = low[1].astype(BF16)
            mid2[2 * mat + 1] = high[3].astype(BF16)
            keep2[2 * mat] = low[0]
            keep2[2 * mat + 1] = high[0]


def third_kernel(*refs):
    ins, outs = refs[:-4], refs[-4:]
    for axis in range(2):
        mid2, up2, down2 = ins[axis * 3 : axis * 3 + 3]
        for mat in range(2):
            outs[axis * 2][mat] = add(mid2[2 * mat], up2[2 * mat]).astype(BF16)
            outs[axis * 2 + 1][mat] = add(mid2[2 * mat + 1], down2[2 * mat]).astype(BF16)


def last_kernel(*refs):
    ins, (grad_up, grad_down) = refs[:-2], refs[-2:]
    width = grad_down.shape[1]
    for axis in range(2):
        keep2, up2, down2, low2, high2 = ins[axis * 5 : axis * 5 + 5]
        for mat in range(2):
            low = add(keep2[2 * mat], down2[2 * mat + 1], low2[mat])
            high = add(keep2[2 * mat + 1], up2[2 * mat + 1], high2[mat])
            for half, value in enumerate((low, high)):
                part = 2 * axis + half
                if mat == 0:
                    grad_down[part * BLOCK : (part + 1) * BLOCK, :] = value
                else:
                    grad_up[:, part * width : (part + 1) * width] = value


def moves(axis, sign):
    pairs = []
    for index in range(SIDE * SIDE):
        y, x = divmod(index, SIDE)
        if axis == 0:
            x = (x + sign) % SIDE
        else:
            y = (y + sign) % SIDE
        pairs.append((index, y * SIDE + x))
    return pairs


def shift(value, axis, sign):
    return lax.ppermute(value, "dp", moves(axis, sign))


def block_places():
    me = lax.axis_index("dp")
    flat = jnp.arange(SIDE * SIDE * 4, dtype=jnp.int32)
    owner, part = flat // 4, flat % 4
    away_x = (owner % SIDE - me % SIDE) % SIDE
    away_y = (owner // SIDE - me // SIDE) % SIDE
    axis, half = part // 2, part % 2
    first = jnp.where(axis == 0, away_x, away_y)
    inner = jnp.where(axis == 0, away_y, away_x)
    role = jnp.zeros_like(flat)
    for h in range(2):
        for d in range(SIDE):
            role = jnp.where((half == h) & (first == d), ROLE[h][d], role)
    return (axis * 8 + role) * SIDE + inner


def params(*semantics, limit=60):
    return pltpu.CompilerParams(
        dimension_semantics=semantics or None, vmem_limit_bytes=limit * 1024 * 1024
    )


def cost(flops, size):
    return pl.CostEstimate(flops=flops, bytes_accessed=size, transcendentals=0)


def whole(shape):
    return pl.BlockSpec(shape, lambda *_: (0,) * len(shape))


ANY = pl.BlockSpec(memory_space=pl.ANY)


def per_device(mix_input, out_grad, w_up, w_down, gain_first, gain_second, owner_dev, slot_row):
    rows, _, width = mix_input.shape
    hidden_units = w_up.shape[2]
    chunk = hidden_units // SIDE
    owners = lax.axis_size("dp")
    pieces = lax.axis_size("token")
    mix, out_g = mix_input.reshape(rows, width), out_grad.reshape(rows, width)
    up_mat, down_mat = w_up[0], w_down[0]
    dest = block_places()
    group = jax.ShapeDtypeStruct((8, BLOCK, width), BF16)
    tall = whole((rows, width))
    gain = whole((1, width))
    clamp = lambda i: jnp.minimum(i, SIDE - 1)
    stage = [pltpu.VMEM((64, BLOCK, width), BF16), pltpu.SemaphoreType.DMA((8,))]
    matmul = 2 * rows * width * hidden_units
    hidden, slope, grad_wide, grad_mid, *down_parts = pl.pallas_call(
        forward_kernel,
        grid_spec=pltpu.PrefetchScalarGridSpec(
            num_scalar_prefetch=1,
            grid=(2 * SIDE,),
            in_specs=[
                tall,
                tall,
                pl.BlockSpec((width, chunk), lambda i, _: (0, clamp(i))),
                pl.BlockSpec((chunk, width), lambda i, _: (clamp(i), 0)),
                gain,
                gain,
            ],
            out_specs=[
                tall,
                pl.BlockSpec((1, rows, chunk), lambda i, _: (clamp(i), 0, 0)),
                tall,
                tall,
            ]
            + [ANY] * 8,
            scratch_shapes=[pltpu.VMEM((SIDE, rows, chunk), BF16)] + stage,
        ),
        out_shape=[
            jax.ShapeDtypeStruct((rows, width), BF16),
            jax.ShapeDtypeStruct((SIDE, rows, chunk), F32),
            jax.ShapeDtypeStruct((rows, width), F32),
            jax.ShapeDtypeStruct((rows, width), BF16),
        ]
        + [group] * 8,
        compiler_params=params("arbitrary"),
        cost_estimate=cost(3 * matmul, 25_000_000),
    )(dest, mix, out_g, up_mat, down_mat, gain_first, gain_second)

    down_got = [
        (shift(down_parts[4 * a], a, 1), shift(down_parts[4 * a + 1], a, -1)) for a in range(2)
    ]

    grad_sum, *up_parts = pl.pallas_call(
        backward_kernel,
        grid_spec=pltpu.PrefetchScalarGridSpec(
            num_scalar_prefetch=1,
            grid=(SIDE,),
            in_specs=[
                tall,
                tall,
                pl.BlockSpec((1, rows, chunk), lambda i, _: (i, 0, 0)),
                tall,
                tall,
                pl.BlockSpec((width, chunk), lambda i, _: (0, i)),
                pl.BlockSpec((chunk, width), lambda i, _: (i, 0)),
                gain,
            ],
            out_specs=[whole((width, rows))] + [ANY] * 8,
            scratch_shapes=[pltpu.VMEM((width, rows), BF16), pltpu.VMEM((rows, width), F32)]
            + stage,
        ),
        out_shape=[jax.ShapeDtypeStruct((width, rows), BF16)] + [group] * 8,
        compiler_params=params("arbitrary"),
        cost_estimate=cost(3 * matmul, 25_000_000),
    )(dest, mix, hidden, slope, grad_wide, grad_mid, up_mat, down_mat, gain_first)

    leaving = [up_parts[k] for k in (0, 1, 4, 5)]
    leaving, grad_sum, down_got = lax.optimization_barrier((leaving, grad_sum, down_got))
    up_parts = [*leaving[:2], *up_parts[2:4], *leaving[2:], *up_parts[6:]]
    up_got = [(shift(up_parts[4 * a], a, 1), shift(up_parts[4 * a + 1], a, -1)) for a in range(2)]

    swapped = lax.all_to_all(
        grad_sum.reshape(pieces, width // pieces, rows),
        "token",
        split_axis=0,
        concat_axis=0,
        tiled=True,
    ).reshape(width, rows)

    mats = ((down_parts, down_got), (up_parts, up_got))

    def lines(count, part=0):
        return pl.BlockSpec((count, ROWS, width), lambda i: (part, i, 0))

    def combine(kernel, specs, args, counts, dtypes, name):
        return pl.pallas_call(
            kernel,
            grid=(BLOCK // ROWS,),
            in_specs=specs,
            out_specs=[lines(n) for n in counts],
            out_shape=[
                jax.ShapeDtypeStruct((n, BLOCK, width), t) for n, t in zip(counts, dtypes)
            ],
            compiler_params=params("arbitrary"),
            cost_estimate=cost(1_000_000, 7_000_000),
            name=name,
        )(*args)

    args, specs = [], []
    for a in range(2):
        for parts, got in mats:
            args += [parts[4 * a + 2], *got[a]]
            specs += [lines(8), lines(4), lines(4)]
    both = combine(first_kernel, specs, args, [8] * 4, [BF16] * 4, "first_sums")
    both_got = [shift(both[2 * a + s], a, 1 - 2 * s) for a in range(2) for s in range(2)]

    swapped, _ = lax.optimization_barrier((swapped, both))
    sent = pl.pallas_call(
        seat_kernel,
        out_shape=jax.ShapeDtypeStruct((owners, SEAT, width), BF16),
        compiler_params=params(),
        cost_estimate=cost(2 * owners * SEAT * rows * width, 4_000_000),
    )(grad_sum, swapped, owner_dev.reshape(1, rows), slot_row)
    landed = lax.all_to_all(sent, "dp", split_axis=0, concat_axis=0, tiled=True)

    args, specs = [], []
    for a in range(2):
        for parts, got in mats:
            args += [parts[4 * a + 3], *got[a]]
            specs += [lines(8), lines(4, 1), lines(4, 1)]
        args += both_got[2 * a : 2 * a + 2]
        specs += [lines(8), lines(8)]
    second = combine(
        second_kernel, specs, args, [4] * 8, [BF16, BF16, BF16, F32] * 2, "second_sums"
    )
    second_got = [shift(second[4 * a + s], 1 - a, 1 - 2 * s) for a in range(2) for s in range(2)]

    args = []
    for a in range(2):
        args += [second[4 * a + 2], *second_got[2 * a : 2 * a + 2]]
    third = combine(third_kernel, [lines(4)] * 6, args, [2] * 4, [BF16] * 4, "third_sums")
    third_got = [shift(third[2 * a + s], 1 - a, 1 - 2 * s) for a in range(2) for s in range(2)]

    args = []
    for a in range(2):
        args += [second[4 * a + 3], *second_got[2 * a : 2 * a + 2], *third_got[2 * a : 2 * a + 2]]
    grad_up, grad_down = pl.pallas_call(
        last_kernel,
        out_shape=[
            jax.ShapeDtypeStruct((BLOCK, hidden_units), F32),
            jax.ShapeDtypeStruct((4 * BLOCK, width), F32),
        ],
        compiler_params=params(),
        cost_estimate=cost(1_000_000, 4_000_000),
        name="last_sums",
    )(*args)

    slots_in = landed[:, CAP, :SEAT].astype(jnp.int32) - 1
    placer = (
        lax.broadcasted_iota(jnp.int32, (HOT, owners, SEAT), 0) == slots_in[None]
    ).astype(BF16)
    row_grad = jnp.dot(
        placer.reshape(HOT, owners * SEAT),
        landed.reshape(owners * SEAT, width),
        preferred_element_type=F32,
    )
    return (grad_up[None], grad_down[None], row_grad[None])


def solution(mesh):
    placed = (
        P("dp", "token", None),
        P("dp", "token", None),
        P("token", None, None),
        P("token", None, None),
        P("token", None),
        P("token", None),
        P("token", "dp", None),
        P("token", "dp"),
    )
    return jax.shard_map(
        per_device,
        mesh=mesh,
        in_specs=placed,
        out_specs=(P("token", "dp", None), P("token", "dp", None), P("token", "dp", None)),
        check_vma=False,
    )
```

```python
import functools

import jax
import jax.numpy as jnp
from jax import lax
from jax.experimental import pallas as pl
from jax.experimental.pallas import tpu as pltpu
from jax.sharding import PartitionSpec as P

HOT = 256
CAP = 56
SEAT = 64
SIDE = 4
BLOCK = 48
ROWS = 16

EPS = 1e-05
HALF_ROOT = 0.7071067811865476
INV_ROOT_TAU = 0.3989422804014327
F32 = jnp.float32
BF16 = jnp.bfloat16

ROLE = ((6, 4, 0, 3), (7, 1, 2, 5))


def normalize(values):
    center = values - jnp.mean(values, axis=-1, keepdims=True)
    inv_scale = lax.rsqrt(jnp.mean(center * center, axis=-1, keepdims=True) + EPS)
    return (center * inv_scale, inv_scale)


def norm_back(grad_norm, normed, inv_scale):
    mean_grad = jnp.mean(grad_norm, axis=-1, keepdims=True)
    mean_proj = jnp.mean(grad_norm * normed, axis=-1, keepdims=True)
    return inv_scale * (grad_norm - mean_grad - normed * mean_proj)


def gelu_parts(pre_act):
    cumul = 0.5 * (1.0 + lax.erf(pre_act * HALF_ROOT))
    density = jnp.exp(-0.5 * pre_act * pre_act) * INV_ROOT_TAU
    return (pre_act * cumul, cumul + pre_act * density)


def contract_rows(left, right):
    return lax.dot_general(left, right, (((0,), (0,)), ((), ())), preferred_element_type=F32)


def contract_cols(left, right):
    return lax.dot_general(left, right, (((1,), (1,)), ((), ())), preferred_element_type=F32)


def send_out(stage, outs, sems):
    copies = [
        pltpu.make_async_copy(stage.at[pl.ds(8 * k, 8)], out, sems.at[k])
        for k, out in enumerate(outs)
    ]
    for copy in copies:
        copy.start()
    for copy in copies:
        copy.wait()


def forward_kernel(mix, out_grad, w_up, w_down, gain_first, gain_second, *refs):
    hidden, slope, grad_wide, grad_mid, grad_down, active = refs
    step = pl.program_id(0)

    @pl.when(step == 0)
    def _():
        normed, _ = normalize(mix[...].astype(F32))
        hidden[...] = (normed * gain_first[...]).astype(BF16)

    @pl.when(step < SIDE)
    def _():
        pre_act = jnp.dot(hidden[...], w_up[...], preferred_element_type=F32)
        act_value, act_slope = gelu_parts(pre_act)
        act_value = act_value.astype(BF16)
        active[step] = act_value
        slope[0] = act_slope
        part = jnp.dot(act_value, w_down[...], preferred_element_type=F32)

        @pl.when(step == 0)
        def _():
            grad_wide[...] = part + hidden[...].astype(F32)

        @pl.when(step > 0)
        def _():
            grad_wide[...] += part

    @pl.when(step == SIDE - 1)
    def _():
        normed_out, inv_out = normalize(grad_wide[...])
        wide = norm_back(out_grad[...].astype(F32) * gain_second[...], normed_out, inv_out)
        grad_wide[...] = wide
        grad_mid[...] = wide.astype(BF16)

    @pl.when(step >= SIDE)
    def _():
        grad_down[...] = contract_rows(active[step - SIDE], grad_mid[...]).astype(BF16)


def backward_kernel(
    dest, mix, hidden, slope, grad_wide, grad_mid, w_up, w_down, gain_first, *refs
):
    grad_sum, outs = refs[0], refs[1:9]
    turned, grad_hidden, stage, sems = refs[9:]
    step = pl.program_id(0)

    @pl.when(step == 0)
    def _():
        turned[...] = hidden[...].T

    grad_act = contract_cols(grad_mid[...], w_down[...])
    grad_pre = (grad_act * slope[0]).astype(BF16)
    part = jnp.dot(turned[...], grad_pre, preferred_element_type=F32).astype(BF16)
    for k in range(16):
        stage[dest[k * 4 + step]] = part[k * BLOCK : (k + 1) * BLOCK]
    part = contract_cols(grad_pre, w_up[...])

    @pl.when(step == 0)
    def _():
        grad_hidden[...] = part + grad_wide[...]

    @pl.when(step > 0)
    def _():
        grad_hidden[...] += part

    @pl.when(step == SIDE - 1)
    def _():
        normed, inv_scale = normalize(mix[...].astype(F32))
        total = norm_back(grad_hidden[...] * gain_first[...], normed, inv_scale)
        grad_sum[...] = total.T.astype(BF16)
        send_out(stage, outs, sems)


def seat_kernel(grad_sum, swapped, owner, slot, sent):
    owners, rows = sent.shape[0], owner.shape[1]
    width = sent.shape[2]
    iota = functools.partial(lax.broadcasted_iota, jnp.int32)
    embed = (grad_sum[...].astype(F32) + swapped[...].astype(F32)).astype(BF16)
    owner_hot = iota((owners, rows), 0) == owner[...]
    earlier = (iota((rows, rows), 0) < iota((rows, rows), 1)).astype(F32).astype(BF16)
    ahead = jnp.dot(
        owner_hot.astype(F32).astype(BF16), earlier, preferred_element_type=F32
    )
    rank = jnp.sum(jnp.where(owner_hot, ahead, 0.0), axis=0, keepdims=True).astype(jnp.int32)
    rank_hot = (iota((width, rows), 0) == rank).astype(F32).astype(BF16)
    slot_next = jnp.where(owner_hot, (slot[...] + 1).astype(F32), 0.0).astype(BF16)
    slots = contract_cols(slot_next, rank_hot)
    seat = owner[...] * SEAT + rank
    picker = (iota((owners * SEAT, rows), 0) == seat).astype(F32).astype(BF16)
    chosen = contract_cols(picker, embed).reshape(owners, SEAT, width)
    at_cap = iota((1, SEAT, 1), 1) == CAP
    sent[...] = jnp.where(at_cap, slots[:, None, :], chosen).astype(BF16)


def add(*refs):
    total = refs[0].astype(F32)
    for ref in refs[1:]:
        total = total + ref.astype(F32)
    return total


def first_kernel(*refs):
    ins, outs = refs[:-4], refs[-4:]
    for axis in range(2):
        keep, up, down = ins[axis * 3 : axis * 3 + 3]
        outs[axis * 2][...] = add(keep[:SIDE], up[...]).astype(BF16)
        outs[axis * 2 + 1][...] = add(keep[SIDE:], down[...]).astype(BF16)


def second_kernel(*refs):
    ins, outs = refs[:-8], refs[-8:]
    for axis in range(2):
        keep, up, down, low, high = ins[axis * 5 : axis * 5 + 5]
        totals = add(keep[:SIDE], down[...], low[...]), add(keep[SIDE:], up[...], high[...])
        for half, total in enumerate(totals):
            for away in range(SIDE):
                out = outs[axis * 4 + away]
                out[half] = total[away].astype(out.dtype)


def last_kernel(*refs):
    ins, grad_up = refs[:-1], refs[-1]
    width = grad_up.shape[1] // SIDE
    for axis in range(2):
        for half in range(2):
            part = 2 * axis + half
            total = add(*(ref[half] for ref in ins[axis * 4 : axis * 4 + 4]))
            grad_up[:, part * width : (part + 1) * width] = total


def moves(axis, sign):
    pairs = []
    for index in range(SIDE * SIDE):
        y, x = divmod(index, SIDE)
        if axis == 0:
            x = (x + sign) % SIDE
        else:
            y = (y + sign) % SIDE
        pairs.append((index, y * SIDE + x))
    return pairs


def shift(value, axis, sign):
    return lax.ppermute(value, "dp", moves(axis, sign))


def block_places():
    me = lax.axis_index("dp")
    flat = jnp.arange(SIDE * SIDE * 4, dtype=jnp.int32)
    owner, part = flat // 4, flat % 4
    away_x = (owner % SIDE - me % SIDE) % SIDE
    away_y = (owner // SIDE - me // SIDE) % SIDE
    axis, half = part // 2, part % 2
    first = jnp.where(axis == 0, away_x, away_y)
    inner = jnp.where(axis == 0, away_y, away_x)
    role = jnp.zeros_like(flat)
    for h in range(2):
        for d in range(SIDE):
            role = jnp.where((half == h) & (first == d), ROLE[h][d], role)
    return (axis * 8 + role) * SIDE + inner


def params(*semantics, limit=60):
    return pltpu.CompilerParams(
        dimension_semantics=semantics or None, vmem_limit_bytes=limit * 1024 * 1024
    )


def cost(flops, size):
    return pl.CostEstimate(flops=flops, bytes_accessed=size, transcendentals=0)


def whole(shape):
    return pl.BlockSpec(shape, lambda *_: (0,) * len(shape))


ANY = pl.BlockSpec(memory_space=pl.ANY)


def per_device(mix_input, out_grad, w_up, w_down, gain_first, gain_second, owner_dev, slot_row):
    rows, _, width = mix_input.shape
    hidden_units = w_up.shape[2]
    chunk = hidden_units // SIDE
    owners = lax.axis_size("dp")
    pieces = lax.axis_size("token")
    mix, out_g = mix_input.reshape(rows, width), out_grad.reshape(rows, width)
    up_mat, down_mat = w_up[0], w_down[0]
    dest = block_places()
    group = jax.ShapeDtypeStruct((8, BLOCK, width), BF16)
    tall = whole((rows, width))
    gain = whole((1, width))
    clamp = lambda i: jnp.minimum(i, SIDE - 1)
    stage = [pltpu.VMEM((64, BLOCK, width), BF16), pltpu.SemaphoreType.DMA((8,))]
    matmul = 2 * rows * width * hidden_units
    hidden, slope, grad_wide, grad_mid, down_whole = pl.pallas_call(
        forward_kernel,
        grid=(2 * SIDE,),
        in_specs=[
            tall,
            tall,
            pl.BlockSpec((width, chunk), lambda i: (0, clamp(i))),
            pl.BlockSpec((chunk, width), lambda i: (clamp(i), 0)),
            gain,
            gain,
        ],
        out_specs=[
            tall,
            pl.BlockSpec((1, rows, chunk), lambda i: (clamp(i), 0, 0)),
            tall,
            tall,
            pl.BlockSpec((chunk, width), lambda i: (jnp.maximum(i - SIDE, 0), 0)),
        ],
        out_shape=[
            jax.ShapeDtypeStruct((rows, width), BF16),
            jax.ShapeDtypeStruct((SIDE, rows, chunk), F32),
            jax.ShapeDtypeStruct((rows, width), F32),
            jax.ShapeDtypeStruct((rows, width), BF16),
            jax.ShapeDtypeStruct((hidden_units, width), BF16),
        ],
        scratch_shapes=[pltpu.VMEM((SIDE, rows, chunk), BF16)],
        compiler_params=params("arbitrary"),
        cost_estimate=cost(3 * matmul, 25_000_000),
        name="forward_and_grad_down",
    )(mix, out_g, up_mat, down_mat, gain_first, gain_second)

    grad_down = lax.psum_scatter(down_whole, "dp", scatter_dimension=0, tiled=True).astype(F32)

    grad_sum, *up_parts = pl.pallas_call(
        backward_kernel,
        grid_spec=pltpu.PrefetchScalarGridSpec(
            num_scalar_prefetch=1,
            grid=(SIDE,),
            in_specs=[
                tall,
                tall,
                pl.BlockSpec((1, rows, chunk), lambda i, _: (i, 0, 0)),
                tall,
                tall,
                pl.BlockSpec((width, chunk), lambda i, _: (0, i)),
                pl.BlockSpec((chunk, width), lambda i, _: (i, 0)),
                gain,
            ],
            out_specs=[whole((width, rows))] + [ANY] * 8,
            scratch_shapes=[pltpu.VMEM((width, rows), BF16), pltpu.VMEM((rows, width), F32)]
            + stage,
        ),
        out_shape=[jax.ShapeDtypeStruct((width, rows), BF16)] + [group] * 8,
        compiler_params=params("arbitrary"),
        cost_estimate=cost(3 * matmul, 25_000_000),
        name="backward_and_grad_up",
    )(dest, mix, hidden, slope, grad_wide, grad_mid, up_mat, down_mat, gain_first)

    got = [(shift(up_parts[4 * a], a, 1), shift(up_parts[4 * a + 1], a, -1)) for a in range(2)]

    swapped = lax.all_to_all(
        grad_sum.reshape(pieces, width // pieces, rows),
        "token",
        split_axis=0,
        concat_axis=0,
        tiled=True,
    ).reshape(width, rows)

    def lines(count, part=0):
        return pl.BlockSpec((count, ROWS, width), lambda i: (part, i, 0))

    def combine(kernel, specs, args, counts, dtypes, name):
        return pl.pallas_call(
            kernel,
            grid=(BLOCK // ROWS,),
            in_specs=specs,
            out_specs=[lines(n) for n in counts],
            out_shape=[
                jax.ShapeDtypeStruct((n, BLOCK, width), t) for n, t in zip(counts, dtypes)
            ],
            compiler_params=params("arbitrary"),
            cost_estimate=cost(1_000_000, 7_000_000),
            name=name,
        )(*args)

    args = []
    for a in range(2):
        args += [up_parts[4 * a + 2], *got[a]]
    specs = [lines(8), lines(4), lines(4)] * 2
    passed = combine(first_kernel, specs, args, [4] * 4, [BF16] * 4, "first_sums")
    passed_got = [shift(passed[2 * a + s], a, 1 - 2 * s) for a in range(2) for s in range(2)]

    swapped, _ = lax.optimization_barrier((swapped, passed))
    sent = pl.pallas_call(
        seat_kernel,
        out_shape=jax.ShapeDtypeStruct((owners, SEAT, width), BF16),
        compiler_params=params(),
        cost_estimate=cost(2 * owners * SEAT * rows * width, 4_000_000),
    )(grad_sum, swapped, owner_dev.reshape(1, rows), slot_row)
    landed = lax.all_to_all(sent, "dp", split_axis=0, concat_axis=0, tiled=True)

    args = []
    for a in range(2):
        args += [up_parts[4 * a + 3], *got[a], *passed_got[2 * a : 2 * a + 2]]
    specs = [lines(8), lines(4, 1), lines(4, 1), lines(4), lines(4)] * 2
    lined = combine(
        second_kernel, specs, args, [2] * 8, [F32, BF16, BF16, BF16] * 2, "second_sums"
    )
    args = []
    for a in range(2):
        args += [lined[4 * a]]
        args += [shift(lined[4 * a + away], 1 - a, away) for away in range(1, SIDE)]
    grad_up = pl.pallas_call(
        last_kernel,
        out_shape=jax.ShapeDtypeStruct((BLOCK, hidden_units), F32),
        compiler_params=params(),
        cost_estimate=cost(1_000_000, 2_000_000),
        name="last_sums",
    )(*args)

    slots_in = landed[:, CAP, :SEAT].astype(jnp.int32) - 1
    placer = (
        lax.broadcasted_iota(jnp.int32, (HOT, owners, SEAT), 0) == slots_in[None]
    ).astype(BF16)
    row_grad = jnp.dot(
        placer.reshape(HOT, owners * SEAT),
        landed.reshape(owners * SEAT, width),
        preferred_element_type=F32,
    )
    return (grad_up[None], grad_down[None], row_grad[None])


def solution(mesh):
    placed = (
        P("dp", "token", None),
        P("dp", "token", None),
        P("token", None, None),
        P("token", None, None),
        P("token", None),
        P("token", None),
        P("token", "dp", None),
        P("token", "dp"),
    )
    return jax.shard_map(
        per_device,
        mesh=mesh,
        in_specs=placed,
        out_specs=(P("token", "dp", None), P("token", "dp", None), P("token", "dp", None)),
        check_vma=False,
    )
```

```python
import functools

import jax
import jax.numpy as jnp
from jax import lax
from jax.experimental import pallas as pl
from jax.experimental.pallas import tpu as pltpu
from jax.sharding import PartitionSpec as P

HOT = 256
CAP = 56
SEAT = 64
SIDE = 4
BLOCK = 48
ROWS = 16

EPS = 1e-05
HALF_ROOT = 0.7071067811865476
INV_ROOT_TAU = 0.3989422804014327
F32 = jnp.float32
BF16 = jnp.bfloat16


def normalize(values):
    center = values - jnp.mean(values, axis=-1, keepdims=True)
    inv_scale = lax.rsqrt(jnp.mean(center * center, axis=-1, keepdims=True) + EPS)
    return (center * inv_scale, inv_scale)


def norm_back(grad_norm, normed, inv_scale):
    mean_grad = jnp.mean(grad_norm, axis=-1, keepdims=True)
    mean_proj = jnp.mean(grad_norm * normed, axis=-1, keepdims=True)
    return inv_scale * (grad_norm - mean_grad - normed * mean_proj)


def gelu_parts(pre_act):
    cumul = 0.5 * (1.0 + lax.erf(pre_act * HALF_ROOT))
    density = jnp.exp(-0.5 * pre_act * pre_act) * INV_ROOT_TAU
    return (pre_act * cumul, cumul + pre_act * density)


def contract_rows(left, right):
    return lax.dot_general(left, right, (((0,), (0,)), ((), ())), preferred_element_type=F32)


def contract_cols(left, right):
    return lax.dot_general(left, right, (((1,), (1,)), ((), ())), preferred_element_type=F32)


def send_out(stage, outs, sems):
    copies = [
        pltpu.make_async_copy(stage.at[pl.ds(8 * k, 8)], out, sems.at[k, 0])
        for k, out in enumerate(outs)
    ]
    for copy in copies:
        copy.start()
    for copy in copies:
        copy.wait()


def send_out(stage, outs, sems):
    copies = [
        pltpu.make_async_copy(stage.at[pl.ds(8 * k, 8)], out, sems.at[k, 0])
        for k, out in enumerate(outs)
    ]
    for copy in copies:
        copy.start()
    for copy in copies:
        copy.wait()


def forward_kernel(dest, mix, out_grad, w_up, w_down, gain_first, gain_second, *refs):
    hidden, slope, grad_wide, grad_mid = refs[:4]
    outs, (active, stage, sems) = refs[4:12], refs[12:]
    step = pl.program_id(0)

    @pl.when(step == 0)
    def _():
        normed, _ = normalize(mix[...].astype(F32))
        hidden[...] = (normed * gain_first[...]).astype(BF16)

    @pl.when(step < SIDE)
    def _():
        pre_act = jnp.dot(hidden[...], w_up[...], preferred_element_type=F32)
        act_value, act_slope = gelu_parts(pre_act)
        act_value = act_value.astype(BF16)
        active[step] = act_value
        slope[0] = act_slope
        part = jnp.dot(act_value, w_down[...], preferred_element_type=F32)

        @pl.when(step == 0)
        def _():
            grad_wide[...] = part + hidden[...].astype(F32)

        @pl.when(step > 0)
        def _():
            grad_wide[...] += part

    @pl.when(step == SIDE - 1)
    def _():
        normed_out, inv_out = normalize(grad_wide[...])
        wide = norm_back(out_grad[...].astype(F32) * gain_second[...], normed_out, inv_out)
        grad_wide[...] = wide
        grad_mid[...] = wide.astype(BF16)

    @pl.when(step >= SIDE)
    def _():
        part = contract_rows(active[step - SIDE], grad_mid[...]).astype(BF16)
        for k in range(16):
            stage[dest[(step - SIDE) * 16 + k]] = part[k * BLOCK : (k + 1) * BLOCK]

    @pl.when(step == 2 * SIDE - 1)
    def _():
        send_out(stage, outs, sems)


def backward_kernel(
    dest, mix, hidden, slope, grad_wide, grad_mid, w_up, w_down, gain_first, *refs
):
    grad_sum, outs = refs[0], refs[1:9]
    turned, grad_hidden, stage, sems = refs[9:]
    step = pl.program_id(0)

    def copies(part):
        axis, half = part // 2, part % 2
        return [
            pltpu.make_async_copy(
                stage.at[pl.ds((k * 2 + half) * SIDE, SIDE)],
                outs[k].at[pl.ds(half * SIDE, SIDE)],
                sems.at[k, half],
            )
            for k in range(axis * SIDE, (axis + 1) * SIDE)
        ]

    @pl.when(step == 0)
    def _():
        turned[...] = hidden[...].T

    grad_act = contract_cols(grad_mid[...], w_down[...])
    grad_pre = (grad_act * slope[0]).astype(BF16)
    part = jnp.dot(turned[...], grad_pre, preferred_element_type=F32).astype(BF16)
    for k in range(16):
        stage[dest[k * 4 + step]] = part[k * BLOCK : (k + 1) * BLOCK]
    for q in range(SIDE):

        @pl.when(step == q)
        def _():
            for copy in copies(q):
                copy.start()

    part = contract_cols(grad_pre, w_up[...])

    @pl.when(step == 0)
    def _():
        grad_hidden[...] = part + grad_wide[...]

    @pl.when(step > 0)
    def _():
        grad_hidden[...] += part

    @pl.when(step == SIDE - 1)
    def _():
        normed, inv_scale = normalize(mix[...].astype(F32))
        total = norm_back(grad_hidden[...] * gain_first[...], normed, inv_scale)
        grad_sum[...] = total.T.astype(BF16)
        for q in range(SIDE):
            for copy in copies(q):
                copy.wait()


def seat_kernel(grad_sum, swapped, owner, slot, sent):
    owners, rows = sent.shape[0], owner.shape[1]
    width = sent.shape[2]
    iota = functools.partial(lax.broadcasted_iota, jnp.int32)
    embed = (grad_sum[...].astype(F32) + swapped[...].astype(F32)).astype(BF16)
    owner_hot = iota((owners, rows), 0) == owner[...]
    earlier = (iota((rows, rows), 0) < iota((rows, rows), 1)).astype(F32).astype(BF16)
    ahead = jnp.dot(
        owner_hot.astype(F32).astype(BF16), earlier, preferred_element_type=F32
    )
    rank = jnp.sum(jnp.where(owner_hot, ahead, 0.0), axis=0, keepdims=True).astype(jnp.int32)
    rank_hot = (iota((width, rows), 0) == rank).astype(F32).astype(BF16)
    slot_next = jnp.where(owner_hot, (slot[...] + 1).astype(F32), 0.0).astype(BF16)
    slots = contract_cols(slot_next, rank_hot)
    seat = owner[...] * SEAT + rank
    picker = (iota((owners * SEAT, rows), 0) == seat).astype(F32).astype(BF16)
    chosen = contract_cols(picker, embed).reshape(owners, SEAT, width)
    at_cap = iota((1, SEAT, 1), 1) == CAP
    sent[...] = jnp.where(at_cap, slots[:, None, :], chosen).astype(BF16)


def add(*refs):
    total = refs[0].astype(F32)
    for ref in refs[1:]:
        total = total + ref.astype(F32)
    return total


def line_kernel(*refs):
    ins, outs = refs[:8], refs[-8:]
    for axis in range(2):
        total = add(*(ref[...] for ref in ins[axis * SIDE : (axis + 1) * SIDE]))
        for half in range(2):
            for away in range(SIDE):
                out = outs[axis * SIDE + away]
                out[half] = total[half * SIDE + away].astype(out.dtype)


def last_kernel(*refs):
    ins, (grad_up, grad_down) = refs[:-2], refs[-2:]
    width = grad_down.shape[1]
    for axis in range(2):
        for half in range(2):
            part = 2 * axis + half
            here = ins[axis * SIDE : (axis + 1) * SIDE]
            grad_down[part * BLOCK : (part + 1) * BLOCK, :] = add(*(ref[half] for ref in here))
            grad_up[:, part * width : (part + 1) * width] = add(*(ref[2 + half] for ref in here))


def moves(axis, sign):
    pairs = []
    for index in range(SIDE * SIDE):
        y, x = divmod(index, SIDE)
        if axis == 0:
            x = (x + sign) % SIDE
        else:
            y = (y + sign) % SIDE
        pairs.append((index, y * SIDE + x))
    return pairs


def shift(value, axis, sign):
    return lax.ppermute(value, "dp", moves(axis, sign))


def block_places():
    me = lax.axis_index("dp")
    flat = jnp.arange(SIDE * SIDE * 4, dtype=jnp.int32)
    owner, part = flat // 4, flat % 4
    away_x = (owner % SIDE - me % SIDE) % SIDE
    away_y = (owner // SIDE - me // SIDE) % SIDE
    axis, half = part // 2, part % 2
    first = jnp.where(axis == 0, away_x, away_y)
    inner = jnp.where(axis == 0, away_y, away_x)
    return ((axis * SIDE + first) * 2 + half) * SIDE + inner


def params(*semantics, limit=60):
    return pltpu.CompilerParams(
        dimension_semantics=semantics or None, vmem_limit_bytes=limit * 1024 * 1024
    )


def cost(flops, size):
    return pl.CostEstimate(flops=flops, bytes_accessed=size, transcendentals=0)


def whole(shape):
    return pl.BlockSpec(shape, lambda *_: (0,) * len(shape))


ANY = pl.BlockSpec(memory_space=pl.ANY)


def per_device(mix_input, out_grad, w_up, w_down, gain_first, gain_second, owner_dev, slot_row):
    rows, _, width = mix_input.shape
    hidden_units = w_up.shape[2]
    chunk = hidden_units // SIDE
    owners = lax.axis_size("dp")
    pieces = lax.axis_size("token")
    mix, out_g = mix_input.reshape(rows, width), out_grad.reshape(rows, width)
    up_mat, down_mat = w_up[0], w_down[0]
    dest = block_places()
    group = jax.ShapeDtypeStruct((8, BLOCK, width), BF16)
    tall = whole((rows, width))
    gain = whole((1, width))
    clamp = lambda i: jnp.minimum(i, SIDE - 1)
    stage = [pltpu.VMEM((64, BLOCK, width), BF16), pltpu.SemaphoreType.DMA((8, 2))]
    matmul = 2 * rows * width * hidden_units
    hidden, slope, grad_wide, grad_mid, *down_parts = pl.pallas_call(
        forward_kernel,
        grid_spec=pltpu.PrefetchScalarGridSpec(
            num_scalar_prefetch=1,
            grid=(2 * SIDE,),
            in_specs=[
                tall,
                tall,
                pl.BlockSpec((width, chunk), lambda i, _: (0, clamp(i))),
                pl.BlockSpec((chunk, width), lambda i, _: (clamp(i), 0)),
                gain,
                gain,
            ],
            out_specs=[
                tall,
                pl.BlockSpec((1, rows, chunk), lambda i, _: (clamp(i), 0, 0)),
                tall,
                tall,
            ]
            + [ANY] * 8,
            scratch_shapes=[pltpu.VMEM((SIDE, rows, chunk), BF16)] + stage,
        ),
        out_shape=[
            jax.ShapeDtypeStruct((rows, width), BF16),
            jax.ShapeDtypeStruct((SIDE, rows, chunk), F32),
            jax.ShapeDtypeStruct((rows, width), F32),
            jax.ShapeDtypeStruct((rows, width), BF16),
        ]
        + [group] * 8,
        compiler_params=params("arbitrary"),
        cost_estimate=cost(3 * matmul, 25_000_000),
        name="forward_and_grad_down",
    )(dest, mix, out_g, up_mat, down_mat, gain_first, gain_second)

    def send(parts, a, away):
        return shift(parts[a * SIDE + away], a, away)

    first_got = [send(down_parts, 0, 1), send(down_parts, 0, 2), send(down_parts, 0, 3)]
    first_got += [send(down_parts, 1, 1), send(down_parts, 1, 3)]

    grad_sum, *up_parts = pl.pallas_call(
        backward_kernel,
        grid_spec=pltpu.PrefetchScalarGridSpec(
            num_scalar_prefetch=1,
            grid=(SIDE,),
            in_specs=[
                tall,
                tall,
                pl.BlockSpec((1, rows, chunk), lambda i, _: (i, 0, 0)),
                tall,
                tall,
                pl.BlockSpec((width, chunk), lambda i, _: (0, i)),
                pl.BlockSpec((chunk, width), lambda i, _: (i, 0)),
                gain,
            ],
            out_specs=[whole((width, rows))] + [ANY] * 8,
            scratch_shapes=[pltpu.VMEM((width, rows), BF16), pltpu.VMEM((rows, width), F32)]
            + stage,
        ),
        out_shape=[jax.ShapeDtypeStruct((width, rows), BF16)] + [group] * 8,
        compiler_params=params("arbitrary"),
        cost_estimate=cost(3 * matmul, 25_000_000),
        name="backward_and_grad_up",
    )(dest, mix, hidden, slope, grad_wide, grad_mid, up_mat, down_mat, gain_first)

    leaving = [up_parts[a * SIDE + away] for a in range(2) for away in range(1, SIDE)]
    leaving, last_down, grad_sum, first_got = lax.optimization_barrier(
        (leaving, down_parts[SIDE + 2], grad_sum, first_got)
    )
    down_got = first_got[:4] + [shift(last_down, 1, 2)] + first_got[4:]
    up_parts = [up_parts[0], *leaving[:3], up_parts[SIDE], *leaving[3:]]
    up_got = [send(up_parts, a, away) for a in range(2) for away in range(1, SIDE)]

    swapped = lax.all_to_all(
        grad_sum.reshape(pieces, width // pieces, rows),
        "token",
        split_axis=0,
        concat_axis=0,
        tiled=True,
    ).reshape(width, rows)

    def lines(count, part=0):
        return pl.BlockSpec((count, ROWS, width), lambda i: (part, i, 0))

    def line_sums(parts, got, mat, before=()):
        return pl.pallas_call(
            line_kernel,
            grid=(BLOCK // ROWS,),
            in_specs=[lines(8)] * 8 + [ANY] * len(before),
            out_specs=[lines(2, mat)] * 8,
            out_shape=[
                jax.ShapeDtypeStruct((4, BLOCK, width), t) for t in [F32, BF16, BF16, BF16] * 2
            ],
            input_output_aliases={8 + k: k for k in range(len(before))},
            compiler_params=params("arbitrary"),
            cost_estimate=cost(1_000_000, 7_000_000),
            name="line_sums",
        )(parts[0], *got[:3], parts[SIDE], *got[3:], *before)

    summed = line_sums(down_parts, down_got, 0)
    swapped, _ = lax.optimization_barrier((swapped, up_got + down_got))
    sent = pl.pallas_call(
        seat_kernel,
        out_shape=jax.ShapeDtypeStruct((owners, SEAT, width), BF16),
        compiler_params=params(),
        cost_estimate=cost(2 * owners * SEAT * rows * width, 4_000_000),
    )(grad_sum, swapped, owner_dev.reshape(1, rows), slot_row)
    landed = lax.all_to_all(sent, "dp", split_axis=0, concat_axis=0, tiled=True)

    summed = line_sums(up_parts, up_got, 1, summed)
    args = []
    for a in range(2):
        args += [summed[a * SIDE]]
        args += [shift(summed[a * SIDE + away], 1 - a, away) for away in range(1, SIDE)]
    grad_up, grad_down = pl.pallas_call(
        last_kernel,
        out_shape=[
            jax.ShapeDtypeStruct((BLOCK, hidden_units), F32),
            jax.ShapeDtypeStruct((4 * BLOCK, width), F32),
        ],
        compiler_params=params(),
        cost_estimate=cost(1_000_000, 4_000_000),
        name="last_sums",
    )(*args)

    slots_in = landed[:, CAP, :SEAT].astype(jnp.int32) - 1
    placer = (
        lax.broadcasted_iota(jnp.int32, (HOT, owners, SEAT), 0) == slots_in[None]
    ).astype(BF16)
    row_grad = jnp.dot(
        placer.reshape(HOT, owners * SEAT),
        landed.reshape(owners * SEAT, width),
        preferred_element_type=F32,
    )
    return (grad_up[None], grad_down[None], row_grad[None])


def solution(mesh):
    placed = (
        P("dp", "token", None),
        P("dp", "token", None),
        P("token", None, None),
        P("token", None, None),
        P("token", None),
        P("token", None),
        P("token", "dp", None),
        P("token", "dp"),
    )
    return jax.shard_map(
        per_device,
        mesh=mesh,
        in_specs=placed,
        out_specs=(P("token", "dp", None), P("token", "dp", None), P("token", "dp", None)),
        check_vma=False,
    )
```

```python
import functools

import jax
import jax.numpy as jnp
from jax import lax
from jax.experimental import pallas as pl
from jax.experimental.pallas import tpu as pltpu
from jax.sharding import PartitionSpec as P

HOT = 256
CAP = 56
SEAT = 64
SIDE = 4
BLOCK = 48
ROWS = 16

EPS = 1e-05
HALF_ROOT = 0.7071067811865476
INV_ROOT_TAU = 0.3989422804014327
F32 = jnp.float32
BF16 = jnp.bfloat16

ROLE = ((6, 4, 0, 3), (7, 1, 2, 5))


def normalize(values):
    center = values - jnp.mean(values, axis=-1, keepdims=True)
    inv_scale = lax.rsqrt(jnp.mean(center * center, axis=-1, keepdims=True) + EPS)
    return (center * inv_scale, inv_scale)


def norm_back(grad_norm, normed, inv_scale):
    mean_grad = jnp.mean(grad_norm, axis=-1, keepdims=True)
    mean_proj = jnp.mean(grad_norm * normed, axis=-1, keepdims=True)
    return inv_scale * (grad_norm - mean_grad - normed * mean_proj)


def gelu_parts(pre_act):
    cumul = 0.5 * (1.0 + lax.erf(pre_act * HALF_ROOT))
    density = jnp.exp(-0.5 * pre_act * pre_act) * INV_ROOT_TAU
    return (pre_act * cumul, cumul + pre_act * density)


def contract_rows(left, right):
    return lax.dot_general(left, right, (((0,), (0,)), ((), ())), preferred_element_type=F32)


def contract_cols(left, right):
    return lax.dot_general(left, right, (((1,), (1,)), ((), ())), preferred_element_type=F32)


def copy_role(stage, outs, axis, role, first, count, sem):
    start = (axis * 8 + role) * SIDE + first
    target = outs[axis * SIDE + role // 2].at[pl.ds(role % 2 * SIDE + first, count)]
    return pltpu.make_async_copy(stage.at[pl.ds(start, count)], target, sem)


def forward_kernel(dest, mix, out_grad, w_up, w_down, gain_first, gain_second, *refs):
    hidden, slope, grad_wide, grad_mid = refs[:4]
    outs, (active, stage, sems) = refs[4:12], refs[12:]
    step = pl.program_id(0)

    @pl.when(step == 0)
    def _():
        normed, _ = normalize(mix[...].astype(F32))
        hidden[...] = (normed * gain_first[...]).astype(BF16)

    @pl.when(step < SIDE)
    def _():
        pre_act = jnp.dot(hidden[...], w_up[...], preferred_element_type=F32)
        act_value, act_slope = gelu_parts(pre_act)
        act_value = act_value.astype(BF16)
        active[step] = act_value
        slope[0] = act_slope
        part = jnp.dot(act_value, w_down[...], preferred_element_type=F32)

        @pl.when(step == 0)
        def _():
            grad_wide[...] = part + hidden[...].astype(F32)

        @pl.when(step > 0)
        def _():
            grad_wide[...] += part

    @pl.when(step == SIDE - 1)
    def _():
        normed_out, inv_out = normalize(grad_wide[...])
        wide = norm_back(out_grad[...].astype(F32) * gain_second[...], normed_out, inv_out)
        grad_wide[...] = wide
        grad_mid[...] = wide.astype(BF16)

    def copies(s):
        whole_lines = [
            copy_role(stage, outs, 1, ROLE[half][s], 0, SIDE, sems.at[s, 8 + half])
            for half in range(2)
        ]
        return whole_lines + [
            copy_role(stage, outs, 0, role, s, 1, sems.at[s, role]) for role in range(8)
        ]

    @pl.when(step >= SIDE)
    def _():
        line = lax.rem(dest[4 * SIDE * SIDE] + step - SIDE, SIDE)
        part = contract_rows(active[line], grad_mid[...]).astype(BF16)
        for k in range(16):
            stage[dest[line * 16 + k]] = part[k * BLOCK : (k + 1) * BLOCK]

    for s in range(SIDE):

        @pl.when(step == SIDE + s)
        def _():
            for copy in copies(s):
                copy.start()

    @pl.when(step == 2 * SIDE - 1)
    def _():
        for s in range(SIDE):
            for copy in copies(s):
                copy.wait()


def grad_up_kernel(dest, hidden, slope, grad_mid, w_down, *refs):
    grad_pre, outs = refs[0], refs[1:9]
    turned, stage, sems = refs[9:]
    step = pl.program_id(0)

    def copies(part):
        axis, half = part // 2, part % 2
        return [
            copy_role(stage, outs, axis, ROLE[half][d], 0, SIDE, sems.at[part, d])
            for d in range(SIDE)
        ]

    @pl.when(step == 0)
    def _():
        turned[...] = hidden[...].T

    value = (contract_cols(grad_mid[...], w_down[...]) * slope[0]).astype(BF16)
    grad_pre[0] = value
    part = jnp.dot(turned[...], value, preferred_element_type=F32).astype(BF16)
    for k in range(16):
        stage[dest[k * 4 + step]] = part[k * BLOCK : (k + 1) * BLOCK]
    for q in range(SIDE):

        @pl.when(step == q)
        def _():
            for copy in copies(q):
                copy.start()

    @pl.when(step == SIDE - 1)
    def _():
        for q in range(SIDE):
            for copy in copies(q):
                copy.wait()


def grad_sum_kernel(mix, grad_pre, grad_wide, w_up, gain_first, grad_sum, grad_hidden):
    step = pl.program_id(0)
    part = contract_cols(grad_pre[0], w_up[...])

    @pl.when(step == 0)
    def _():
        grad_hidden[...] = part + grad_wide[...]

    @pl.when(step > 0)
    def _():
        grad_hidden[...] += part

    @pl.when(step == SIDE - 1)
    def _():
        normed, inv_scale = normalize(mix[...].astype(F32))
        total = norm_back(grad_hidden[...] * gain_first[...], normed, inv_scale)
        grad_sum[...] = total.T.astype(BF16)


def seat_kernel(grad_sum, swapped, owner, slot, sent):
    owners, rows = sent.shape[0], owner.shape[1]
    width = sent.shape[2]
    iota = functools.partial(lax.broadcasted_iota, jnp.int32)
    embed = (grad_sum[...].astype(F32) + swapped[...].astype(F32)).astype(BF16)
    owner_hot = iota((owners, rows), 0) == owner[...]
    earlier = (iota((rows, rows), 0) < iota((rows, rows), 1)).astype(F32).astype(BF16)
    ahead = jnp.dot(
        owner_hot.astype(F32).astype(BF16), earlier, preferred_element_type=F32
    )
    rank = jnp.sum(jnp.where(owner_hot, ahead, 0.0), axis=0, keepdims=True).astype(jnp.int32)
    rank_hot = (iota((width, rows), 0) == rank).astype(F32).astype(BF16)
    slot_next = jnp.where(owner_hot, (slot[...] + 1).astype(F32), 0.0).astype(BF16)
    slots = contract_cols(slot_next, rank_hot)
    seat = owner[...] * SEAT + rank
    picker = (iota((owners * SEAT, rows), 0) == seat).astype(F32).astype(BF16)
    chosen = contract_cols(picker, embed).reshape(owners, SEAT, width)
    at_cap = iota((1, SEAT, 1), 1) == CAP
    sent[...] = jnp.where(at_cap, slots[:, None, :], chosen).astype(BF16)


def add(*refs):
    total = refs[0].astype(F32)
    for ref in refs[1:]:
        total = total + ref.astype(F32)
    return total


def first_kernel(*refs):
    ins, outs = refs[:-4], refs[-4:]
    for axis in range(2):
        for mat in range(2):
            keep, up, down = ins[(axis * 2 + mat) * 3 : (axis * 2 + mat) * 3 + 3]
            rows = pl.ds(mat * SIDE, SIDE)
            outs[axis * 2][rows] = add(keep[:SIDE], up[...]).astype(BF16)
            outs[axis * 2 + 1][rows] = add(keep[SIDE:], down[...]).astype(BF16)


def second_kernel(*refs):
    ins, outs = refs[:-8], refs[-8:]
    for axis in range(2):
        here = ins[axis * 8 : axis * 8 + 8]
        for mat in range(2):
            keep, up, down = here[mat * 3 : mat * 3 + 3]
            rows = slice(mat * SIDE, (mat + 1) * SIDE)
            low = add(keep[:SIDE], down[...], here[6][rows])
            high = add(keep[SIDE:], up[...], here[7][rows])
            for half, total in enumerate((low, high)):
                for away in range(SIDE):
                    out = outs[axis * SIDE + away]
                    out[2 * mat + half] = total[away].astype(out.dtype)


def last_kernel(*refs):
    ins, (grad_up, grad_down) = refs[:-2], refs[-2:]
    width = grad_down.shape[1]
    for axis in range(2):
        for half in range(2):
            part = 2 * axis + half
            here = ins[axis * SIDE : (axis + 1) * SIDE]
            grad_down[part * BLOCK : (part + 1) * BLOCK, :] = add(*(ref[half] for ref in here))
            grad_up[:, part * width : (part + 1) * width] = add(*(ref[2 + half] for ref in here))


def moves(axis, sign):
    pairs = []
    for index in range(SIDE * SIDE):
        y, x = divmod(index, SIDE)
        if axis == 0:
            x = (x + sign) % SIDE
        else:
            y = (y + sign) % SIDE
        pairs.append((index, y * SIDE + x))
    return pairs


def shift(value, axis, sign):
    return lax.ppermute(value, "dp", moves(axis, sign))


def block_places():
    me = lax.axis_index("dp")
    flat = jnp.arange(SIDE * SIDE * 4, dtype=jnp.int32)
    owner, part = flat // 4, flat % 4
    away_x = (owner % SIDE - me % SIDE) % SIDE
    away_y = (owner // SIDE - me // SIDE) % SIDE
    axis, half = part // 2, part % 2
    first = jnp.where(axis == 0, away_x, away_y)
    inner = jnp.where(axis == 0, away_y, away_x)
    role = jnp.zeros_like(flat)
    for h in range(2):
        for d in range(SIDE):
            role = jnp.where((half == h) & (first == d), ROLE[h][d], role)
    places = (axis * 8 + role) * SIDE + inner
    return jnp.concatenate([places, jnp.full((SIDE,), me // SIDE, jnp.int32)])


def params(*semantics, limit=60):
    return pltpu.CompilerParams(
        dimension_semantics=semantics or None, vmem_limit_bytes=limit * 1024 * 1024
    )


def cost(flops, size):
    return pl.CostEstimate(flops=flops, bytes_accessed=size, transcendentals=0)


def whole(shape):
    return pl.BlockSpec(shape, lambda *_: (0,) * len(shape))


ANY = pl.BlockSpec(memory_space=pl.ANY)


def per_device(mix_input, out_grad, w_up, w_down, gain_first, gain_second, owner_dev, slot_row):
    rows, _, width = mix_input.shape
    hidden_units = w_up.shape[2]
    chunk = hidden_units // SIDE
    owners = lax.axis_size("dp")
    pieces = lax.axis_size("token")
    mix, out_g = mix_input.reshape(rows, width), out_grad.reshape(rows, width)
    up_mat, down_mat = w_up[0], w_down[0]
    dest = block_places()
    group = jax.ShapeDtypeStruct((8, BLOCK, width), BF16)
    tall = whole((rows, width))
    gain = whole((1, width))
    clamp = lambda i: jnp.minimum(i, SIDE - 1)
    stage = [pltpu.VMEM((64, BLOCK, width), BF16), pltpu.SemaphoreType.DMA((SIDE, 10))]
    matmul = 2 * rows * width * hidden_units
    hidden, slope, grad_wide, grad_mid, *down_parts = pl.pallas_call(
        forward_kernel,
        grid_spec=pltpu.PrefetchScalarGridSpec(
            num_scalar_prefetch=1,
            grid=(2 * SIDE,),
            in_specs=[
                tall,
                tall,
                pl.BlockSpec((width, chunk), lambda i, _: (0, clamp(i))),
                pl.BlockSpec((chunk, width), lambda i, _: (clamp(i), 0)),
                gain,
                gain,
            ],
            out_specs=[
                tall,
                pl.BlockSpec((1, rows, chunk), lambda i, _: (clamp(i), 0, 0)),
                tall,
                tall,
            ]
            + [ANY] * 8,
            scratch_shapes=[pltpu.VMEM((SIDE, rows, chunk), BF16)] + stage,
        ),
        out_shape=[
            jax.ShapeDtypeStruct((rows, width), BF16),
            jax.ShapeDtypeStruct((SIDE, rows, chunk), F32),
            jax.ShapeDtypeStruct((rows, width), F32),
            jax.ShapeDtypeStruct((rows, width), BF16),
        ]
        + [group] * 8,
        compiler_params=params("arbitrary"),
        cost_estimate=cost(3 * matmul, 25_000_000),
        name="forward_and_grad_down",
    )(dest, mix, out_g, up_mat, down_mat, gain_first, gain_second)

    def send(parts):
        return [(shift(parts[4 * a], a, 1), shift(parts[4 * a + 1], a, -1)) for a in range(2)]

    down_got = send(down_parts)

    grad_pre, *up_parts = pl.pallas_call(
        grad_up_kernel,
        grid_spec=pltpu.PrefetchScalarGridSpec(
            num_scalar_prefetch=1,
            grid=(SIDE,),
            in_specs=[
                tall,
                pl.BlockSpec((1, rows, chunk), lambda i, _: (i, 0, 0)),
                tall,
                pl.BlockSpec((chunk, width), lambda i, _: (i, 0)),
            ],
            out_specs=[pl.BlockSpec((1, rows, chunk), lambda i, _: (i, 0, 0))] + [ANY] * 8,
            scratch_shapes=[pltpu.VMEM((width, rows), BF16)] + stage,
        ),
        out_shape=[jax.ShapeDtypeStruct((SIDE, rows, chunk), BF16)] + [group] * 8,
        compiler_params=params("arbitrary"),
        cost_estimate=cost(2 * matmul, 20_000_000),
        name="grad_pre_and_grad_up",
    )(dest, hidden, slope, grad_mid, down_mat)

    leaving = [up_parts[k] for k in (0, 1, 4, 5)]
    leaving, grad_pre, down_got = lax.optimization_barrier((leaving, grad_pre, down_got))
    up_parts = [*leaving[:2], *up_parts[2:4], *leaving[2:], *up_parts[6:]]
    up_got = send(up_parts)

    grad_sum = pl.pallas_call(
        grad_sum_kernel,
        grid=(SIDE,),
        in_specs=[
            tall,
            pl.BlockSpec((1, rows, chunk), lambda i: (i, 0, 0)),
            tall,
            pl.BlockSpec((width, chunk), lambda i: (0, i)),
            gain,
        ],
        out_specs=whole((width, rows)),
        out_shape=jax.ShapeDtypeStruct((width, rows), BF16),
        scratch_shapes=[pltpu.VMEM((rows, width), F32)],
        compiler_params=params("arbitrary"),
        cost_estimate=cost(matmul, 10_000_000),
        name="grad_sum",
    )(mix, grad_pre, grad_wide, up_mat, gain_first)

    swapped = lax.all_to_all(
        grad_sum.reshape(pieces, width // pieces, rows),
        "token",
        split_axis=0,
        concat_axis=0,
        tiled=True,
    ).reshape(width, rows)

    mats = ((down_parts, down_got), (up_parts, up_got))

    def lines(count, part=0):
        return pl.BlockSpec((count, ROWS, width), lambda i: (part, i, 0))

    def combine(kernel, specs, args, counts, dtypes, name):
        return pl.pallas_call(
            kernel,
            grid=(BLOCK // ROWS,),
            in_specs=specs,
            out_specs=[lines(n) for n in counts],
            out_shape=[
                jax.ShapeDtypeStruct((n, BLOCK, width), t) for n, t in zip(counts, dtypes)
            ],
            compiler_params=params("arbitrary"),
            cost_estimate=cost(1_000_000, 7_000_000),
            name=name,
        )(*args)

    args, specs = [], []
    for a in range(2):
        for parts, got in mats:
            args += [parts[4 * a + 2], *got[a]]
            specs += [lines(8), lines(4), lines(4)]
    both = combine(first_kernel, specs, args, [8] * 4, [BF16] * 4, "first_sums")
    both_got = [shift(both[2 * a + s], a, 1 - 2 * s) for a in range(2) for s in range(2)]

    swapped, _ = lax.optimization_barrier((swapped, both))
    sent = pl.pallas_call(
        seat_kernel,
        out_shape=jax.ShapeDtypeStruct((owners, SEAT, width), BF16),
        compiler_params=params(),
        cost_estimate=cost(2 * owners * SEAT * rows * width, 4_000_000),
    )(grad_sum, swapped, owner_dev.reshape(1, rows), slot_row)
    sent, both_got = lax.optimization_barrier((sent, both_got))
    landed = lax.all_to_all(sent, "dp", split_axis=0, concat_axis=0, tiled=True)

    args, specs = [], []
    for a in range(2):
        for parts, got in mats:
            args += [parts[4 * a + 3], *got[a]]
            specs += [lines(8), lines(4, 1), lines(4, 1)]
        args += both_got[2 * a : 2 * a + 2]
        specs += [lines(8), lines(8)]
    summed = combine(
        second_kernel, specs, args, [4] * 8, [F32, BF16, BF16, BF16] * 2, "second_sums"
    )
    args = []
    for a in range(2):
        args += [summed[a * SIDE]]
        args += [shift(summed[a * SIDE + away], 1 - a, away) for away in range(1, SIDE)]
    grad_up, grad_down = pl.pallas_call(
        last_kernel,
        out_shape=[
            jax.ShapeDtypeStruct((BLOCK, hidden_units), F32),
            jax.ShapeDtypeStruct((4 * BLOCK, width), F32),
        ],
        compiler_params=params(),
        cost_estimate=cost(1_000_000, 4_000_000),
        name="last_sums",
    )(*args)

    slots_in = landed[:, CAP, :SEAT].astype(jnp.int32) - 1
    placer = (
        lax.broadcasted_iota(jnp.int32, (HOT, owners, SEAT), 0) == slots_in[None]
    ).astype(BF16)
    row_grad = jnp.dot(
        placer.reshape(HOT, owners * SEAT),
        landed.reshape(owners * SEAT, width),
        preferred_element_type=F32,
    )
    return (grad_up[None], grad_down[None], row_grad[None])


def solution(mesh):
    placed = (
        P("dp", "token", None),
        P("dp", "token", None),
        P("token", None, None),
        P("token", None, None),
        P("token", None),
        P("token", None),
        P("token", "dp", None),
        P("token", "dp"),
    )
    return jax.shard_map(
        per_device,
        mesh=mesh,
        in_specs=placed,
        out_specs=(P("token", "dp", None), P("token", "dp", None), P("token", "dp", None)),
        check_vma=False,
    )
```

```python
import functools

import jax
import jax.numpy as jnp
from jax import lax
from jax.experimental import pallas as pl
from jax.experimental.pallas import tpu as pltpu
from jax.sharding import PartitionSpec as P

HOT = 256
CAP = 56
SEAT = 64
SIDE = 4
BLOCK = 48
ROWS = 16

EPS = 1e-05
HALF_ROOT = 0.7071067811865476
INV_ROOT_TAU = 0.3989422804014327
F32 = jnp.float32
BF16 = jnp.bfloat16

ROLE = ((6, 4, 0, 3), (7, 1, 2, 5))


def normalize(values):
    center = values - jnp.mean(values, axis=-1, keepdims=True)
    inv_scale = lax.rsqrt(jnp.mean(center * center, axis=-1, keepdims=True) + EPS)
    return (center * inv_scale, inv_scale)


def norm_back(grad_norm, normed, inv_scale):
    mean_grad = jnp.mean(grad_norm, axis=-1, keepdims=True)
    mean_proj = jnp.mean(grad_norm * normed, axis=-1, keepdims=True)
    return inv_scale * (grad_norm - mean_grad - normed * mean_proj)


def gelu_parts(pre_act):
    cumul = 0.5 * (1.0 + lax.erf(pre_act * HALF_ROOT))
    density = jnp.exp(-0.5 * pre_act * pre_act) * INV_ROOT_TAU
    return (pre_act * cumul, cumul + pre_act * density)


def contract_rows(left, right):
    return lax.dot_general(left, right, (((0,), (0,)), ((), ())), preferred_element_type=F32)


def contract_cols(left, right):
    return lax.dot_general(left, right, (((1,), (1,)), ((), ())), preferred_element_type=F32)


def copy_role(stage, outs, axis, role, first, count, sem):
    start = (axis * 8 + role) * SIDE + first
    target = outs[axis * SIDE + role // 2].at[pl.ds(role % 2 * SIDE + first, count)]
    return pltpu.make_async_copy(stage.at[pl.ds(start, count)], target, sem)


def forward_kernel(dest, mix, out_grad, w_up, w_down, gain_first, gain_second, *refs):
    hidden, slope, grad_wide, grad_mid = refs[:4]
    outs, (active, stage, sems) = refs[4:12], refs[12:]
    step = pl.program_id(0)

    @pl.when(step == 0)
    def _():
        normed, _ = normalize(mix[...].astype(F32))
        hidden[...] = (normed * gain_first[...]).astype(BF16)

    @pl.when(step < SIDE)
    def _():
        pre_act = jnp.dot(hidden[...], w_up[...], preferred_element_type=F32)
        act_value, act_slope = gelu_parts(pre_act)
        act_value = act_value.astype(BF16)
        active[step] = act_value
        slope[0] = act_slope
        part = jnp.dot(act_value, w_down[...], preferred_element_type=F32)

        @pl.when(step == 0)
        def _():
            grad_wide[...] = part + hidden[...].astype(F32)

        @pl.when(step > 0)
        def _():
            grad_wide[...] += part

    @pl.when(step == SIDE - 1)
    def _():
        normed_out, inv_out = normalize(grad_wide[...])
        wide = norm_back(out_grad[...].astype(F32) * gain_second[...], normed_out, inv_out)
        grad_wide[...] = wide
        grad_mid[...] = wide.astype(BF16)

    def copies(s):
        whole_lines = [
            copy_role(stage, outs, 1, ROLE[half][s], 0, SIDE, sems.at[s, 8 + half])
            for half in range(2)
        ]
        return whole_lines + [
            copy_role(stage, outs, 0, role, s, 1, sems.at[s, role]) for role in range(8)
        ]

    @pl.when(step >= SIDE)
    def _():
        line = lax.rem(dest[4 * SIDE * SIDE] + step - SIDE, SIDE)
        part = contract_rows(active[line], grad_mid[...]).astype(BF16)
        for k in range(16):
            stage[dest[line * 16 + k]] = part[k * BLOCK : (k + 1) * BLOCK]

    for s in range(SIDE):

        @pl.when(step == SIDE + s)
        def _():
            for copy in copies(s):
                copy.start()

    @pl.when(step == 2 * SIDE - 1)
    def _():
        for s in range(SIDE):
            for copy in copies(s):
                copy.wait()


def backward_kernel(
    dest, mix, hidden, slope, grad_wide, grad_mid, w_up, w_down, gain_first, *refs
):
    grad_sum, outs = refs[0], refs[1:9]
    turned, grad_hidden, stage, sems = refs[9:]
    step = pl.program_id(0)

    def copies(part):
        axis, half = part // 2, part % 2
        return [
            copy_role(stage, outs, axis, ROLE[half][d], 0, SIDE, sems.at[part, d])
            for d in range(SIDE)
        ]

    @pl.when(step == 0)
    def _():
        turned[...] = hidden[...].T

    grad_act = contract_cols(grad_mid[...], w_down[...])
    grad_pre = (grad_act * slope[0]).astype(BF16)
    part = jnp.dot(turned[...], grad_pre, preferred_element_type=F32).astype(BF16)
    for k in range(16):
        stage[dest[k * 4 + step]] = part[k * BLOCK : (k + 1) * BLOCK]
    for q in range(SIDE):

        @pl.when(step == q)
        def _():
            for copy in copies(q):
                copy.start()

    part = contract_cols(grad_pre, w_up[...])

    @pl.when(step == 0)
    def _():
        grad_hidden[...] = part + grad_wide[...]

    @pl.when(step > 0)
    def _():
        grad_hidden[...] += part

    @pl.when(step == SIDE - 1)
    def _():
        normed, inv_scale = normalize(mix[...].astype(F32))
        total = norm_back(grad_hidden[...] * gain_first[...], normed, inv_scale)
        grad_sum[...] = total.T.astype(BF16)
        for q in range(SIDE):
            for copy in copies(q):
                copy.wait()


def seat_kernel(grad_sum, swapped, owner, slot, sent):
    owners, rows = sent.shape[0], owner.shape[1]
    width = sent.shape[2]
    iota = functools.partial(lax.broadcasted_iota, jnp.int32)
    embed = (grad_sum[...].astype(F32) + swapped[...].astype(F32)).astype(BF16)
    owner_hot = iota((owners, rows), 0) == owner[...]
    earlier = (iota((rows, rows), 0) < iota((rows, rows), 1)).astype(F32).astype(BF16)
    ahead = jnp.dot(
        owner_hot.astype(F32).astype(BF16), earlier, preferred_element_type=F32
    )
    rank = jnp.sum(jnp.where(owner_hot, ahead, 0.0), axis=0, keepdims=True).astype(jnp.int32)
    rank_hot = (iota((width, rows), 0) == rank).astype(F32).astype(BF16)
    slot_next = jnp.where(owner_hot, (slot[...] + 1).astype(F32), 0.0).astype(BF16)
    slots = contract_cols(slot_next, rank_hot)
    seat = owner[...] * SEAT + rank
    picker = (iota((owners * SEAT, rows), 0) == seat).astype(F32).astype(BF16)
    chosen = contract_cols(picker, embed).reshape(owners, SEAT, width)
    at_cap = iota((1, SEAT, 1), 1) == CAP
    sent[...] = jnp.where(at_cap, slots[:, None, :], chosen).astype(BF16)


def add(*refs):
    total = refs[0].astype(F32)
    for ref in refs[1:]:
        total = total + ref.astype(F32)
    return total


def first_kernel(*refs):
    ins, outs = refs[:-4], refs[-4:]
    for axis in range(2):
        for mat in range(2):
            keep, up, down = ins[(axis * 2 + mat) * 3 : (axis * 2 + mat) * 3 + 3]
            rows = pl.ds(mat * SIDE, SIDE)
            outs[axis * 2][rows] = add(keep[:SIDE], up[...]).astype(BF16)
            outs[axis * 2 + 1][rows] = add(keep[SIDE:], down[...]).astype(BF16)


def second_kernel(*refs):
    ins, outs = refs[:-8], refs[-8:]
    for axis in range(2):
        here = ins[axis * 8 : axis * 8 + 8]
        for mat in range(2):
            keep, up, down = here[mat * 3 : mat * 3 + 3]
            rows = slice(mat * SIDE, (mat + 1) * SIDE)
            low = add(keep[:SIDE], down[...], here[6][rows])
            high = add(keep[SIDE:], up[...], here[7][rows])
            for half, total in enumerate((low, high)):
                for away in range(SIDE):
                    out = outs[axis * SIDE + away]
                    out[2 * mat + half] = total[away].astype(out.dtype)


def last_kernel(*refs):
    ins, (grad_up, grad_down) = refs[:-2], refs[-2:]
    width = grad_down.shape[1]
    for axis in range(2):
        for half in range(2):
            part = 2 * axis + half
            here = ins[axis * SIDE : (axis + 1) * SIDE]
            grad_down[part * BLOCK : (part + 1) * BLOCK, :] = add(*(ref[half] for ref in here))
            grad_up[:, part * width : (part + 1) * width] = add(*(ref[2 + half] for ref in here))


def moves(axis, sign):
    pairs = []
    for index in range(SIDE * SIDE):
        y, x = divmod(index, SIDE)
        if axis == 0:
            x = (x + sign) % SIDE
        else:
            y = (y + sign) % SIDE
        pairs.append((index, y * SIDE + x))
    return pairs


def shift(value, axis, sign):
    return lax.ppermute(value, "dp", moves(axis, sign))


def block_places():
    me = lax.axis_index("dp")
    flat = jnp.arange(SIDE * SIDE * 4, dtype=jnp.int32)
    owner, part = flat // 4, flat % 4
    away_x = (owner % SIDE - me % SIDE) % SIDE
    away_y = (owner // SIDE - me // SIDE) % SIDE
    axis, half = part // 2, part % 2
    first = jnp.where(axis == 0, away_x, away_y)
    inner = jnp.where(axis == 0, away_y, away_x)
    role = jnp.zeros_like(flat)
    for h in range(2):
        for d in range(SIDE):
            role = jnp.where((half == h) & (first == d), ROLE[h][d], role)
    places = (axis * 8 + role) * SIDE + inner
    return jnp.concatenate([places, jnp.full((SIDE,), me // SIDE, jnp.int32)])


def params(*semantics, limit=60):
    return pltpu.CompilerParams(
        dimension_semantics=semantics or None, vmem_limit_bytes=limit * 1024 * 1024
    )


def cost(flops, size):
    return pl.CostEstimate(flops=flops, bytes_accessed=size, transcendentals=0)


def whole(shape):
    return pl.BlockSpec(shape, lambda *_: (0,) * len(shape))


ANY = pl.BlockSpec(memory_space=pl.ANY)


def per_device(mix_input, out_grad, w_up, w_down, gain_first, gain_second, owner_dev, slot_row):
    rows, _, width = mix_input.shape
    hidden_units = w_up.shape[2]
    chunk = hidden_units // SIDE
    owners = lax.axis_size("dp")
    pieces = lax.axis_size("token")
    mix, out_g = mix_input.reshape(rows, width), out_grad.reshape(rows, width)
    up_mat, down_mat = w_up[0], w_down[0]
    dest = block_places()
    group = jax.ShapeDtypeStruct((8, BLOCK, width), BF16)
    tall = whole((rows, width))
    gain = whole((1, width))
    clamp = lambda i: jnp.minimum(i, SIDE - 1)
    stage = [pltpu.VMEM((64, BLOCK, width), BF16), pltpu.SemaphoreType.DMA((SIDE, 10))]
    matmul = 2 * rows * width * hidden_units
    hidden, slope, grad_wide, grad_mid, *down_parts = pl.pallas_call(
        forward_kernel,
        grid_spec=pltpu.PrefetchScalarGridSpec(
            num_scalar_prefetch=1,
            grid=(2 * SIDE,),
            in_specs=[
                tall,
                tall,
                pl.BlockSpec((width, chunk), lambda i, _: (0, clamp(i))),
                pl.BlockSpec((chunk, width), lambda i, _: (clamp(i), 0)),
                gain,
                gain,
            ],
            out_specs=[
                tall,
                pl.BlockSpec((1, rows, chunk), lambda i, _: (clamp(i), 0, 0)),
                tall,
                tall,
            ]
            + [ANY] * 8,
            scratch_shapes=[pltpu.VMEM((SIDE, rows, chunk), BF16)] + stage,
        ),
        out_shape=[
            jax.ShapeDtypeStruct((rows, width), BF16),
            jax.ShapeDtypeStruct((SIDE, rows, chunk), F32),
            jax.ShapeDtypeStruct((rows, width), F32),
            jax.ShapeDtypeStruct((rows, width), BF16),
        ]
        + [group] * 8,
        compiler_params=params("arbitrary"),
        cost_estimate=cost(3 * matmul, 25_000_000),
        name="forward_and_grad_down",
    )(dest, mix, out_g, up_mat, down_mat, gain_first, gain_second)

    def send(parts):
        return [(shift(parts[4 * a], a, 1), shift(parts[4 * a + 1], a, -1)) for a in range(2)]

    down_got = send(down_parts)

    grad_sum, *up_parts = pl.pallas_call(
        backward_kernel,
        grid_spec=pltpu.PrefetchScalarGridSpec(
            num_scalar_prefetch=1,
            grid=(SIDE,),
            in_specs=[
                tall,
                tall,
                pl.BlockSpec((1, rows, chunk), lambda i, _: (i, 0, 0)),
                tall,
                tall,
                pl.BlockSpec((width, chunk), lambda i, _: (0, i)),
                pl.BlockSpec((chunk, width), lambda i, _: (i, 0)),
                gain,
            ],
            out_specs=[whole((width, rows))] + [ANY] * 8,
            scratch_shapes=[pltpu.VMEM((width, rows), BF16), pltpu.VMEM((rows, width), F32)]
            + stage,
        ),
        out_shape=[jax.ShapeDtypeStruct((width, rows), BF16)] + [group] * 8,
        compiler_params=params("arbitrary"),
        cost_estimate=cost(3 * matmul, 25_000_000),
        name="backward_and_grad_up",
    )(dest, mix, hidden, slope, grad_wide, grad_mid, up_mat, down_mat, gain_first)

    leaving = [up_parts[k] for k in (0, 1, 4, 5)]
    leaving, grad_sum, down_got = lax.optimization_barrier((leaving, grad_sum, down_got))
    up_parts = [*leaving[:2], *up_parts[2:4], *leaving[2:], *up_parts[6:]]
    up_got = send(up_parts)

    swapped = lax.all_to_all(
        grad_sum.reshape(pieces, width // pieces, rows),
        "token",
        split_axis=0,
        concat_axis=0,
        tiled=True,
    ).reshape(width, rows)

    mats = ((down_parts, down_got), (up_parts, up_got))

    def lines(count, part=0):
        return pl.BlockSpec((count, ROWS, width), lambda i: (part, i, 0))

    def combine(kernel, specs, args, counts, dtypes, name):
        return pl.pallas_call(
            kernel,
            grid=(BLOCK // ROWS,),
            in_specs=specs,
            out_specs=[lines(n) for n in counts],
            out_shape=[
                jax.ShapeDtypeStruct((n, BLOCK, width), t) for n, t in zip(counts, dtypes)
            ],
            compiler_params=params("arbitrary"),
            cost_estimate=cost(1_000_000, 7_000_000),
            name=name,
        )(*args)

    args, specs = [], []
    for a in range(2):
        for parts, got in mats:
            args += [parts[4 * a + 2], *got[a]]
            specs += [lines(8), lines(4), lines(4)]
    both = combine(first_kernel, specs, args, [8] * 4, [BF16] * 4, "first_sums")
    both_got = [shift(both[2 * a + s], a, 1 - 2 * s) for a in range(2) for s in range(2)]

    swapped, _ = lax.optimization_barrier((swapped, both))
    sent = pl.pallas_call(
        seat_kernel,
        out_shape=jax.ShapeDtypeStruct((owners, SEAT, width), BF16),
        compiler_params=params(),
        cost_estimate=cost(2 * owners * SEAT * rows * width, 4_000_000),
    )(grad_sum, swapped, owner_dev.reshape(1, rows), slot_row)
    sent, both_got = lax.optimization_barrier((sent, both_got))
    landed = lax.all_to_all(sent, "dp", split_axis=0, concat_axis=0, tiled=True)

    args, specs = [], []
    for a in range(2):
        for parts, got in mats:
            args += [parts[4 * a + 3], *got[a]]
            specs += [lines(8), lines(4, 1), lines(4, 1)]
        args += both_got[2 * a : 2 * a + 2]
        specs += [lines(8), lines(8)]
    summed = combine(
        second_kernel, specs, args, [4] * 8, [F32, BF16, BF16, BF16] * 2, "second_sums"
    )
    args = []
    for a in range(2):
        args += [summed[a * SIDE]]
        args += [shift(summed[a * SIDE + away], 1 - a, away) for away in range(1, SIDE)]
    grad_up, grad_down = pl.pallas_call(
        last_kernel,
        out_shape=[
            jax.ShapeDtypeStruct((BLOCK, hidden_units), F32),
            jax.ShapeDtypeStruct((4 * BLOCK, width), F32),
        ],
        compiler_params=params(),
        cost_estimate=cost(1_000_000, 4_000_000),
        name="last_sums",
    )(*args)

    slots_in = landed[:, CAP, :SEAT].astype(jnp.int32) - 1
    placer = (
        lax.broadcasted_iota(jnp.int32, (HOT, owners, SEAT), 0) == slots_in[None]
    ).astype(BF16)
    row_grad = jnp.dot(
        placer.reshape(HOT, owners * SEAT),
        landed.reshape(owners * SEAT, width),
        preferred_element_type=F32,
    )
    return (grad_up[None], grad_down[None], row_grad[None])


def solution(mesh):
    placed = (
        P("dp", "token", None),
        P("dp", "token", None),
        P("token", None, None),
        P("token", None, None),
        P("token", None),
        P("token", None),
        P("token", "dp", None),
        P("token", "dp"),
    )
    return jax.shard_map(
        per_device,
        mesh=mesh,
        in_specs=placed,
        out_specs=(P("token", "dp", None), P("token", "dp", None), P("token", "dp", None)),
        check_vma=False,
    )
```

```python
import functools

import jax
import jax.numpy as jnp
from jax import lax
from jax.experimental import pallas as pl
from jax.experimental.pallas import tpu as pltpu
from jax.sharding import PartitionSpec as P

HOT = 256
CAP = 56
SEAT = 64
SIDE = 4
BLOCK = 48
ROWS = 48

EPS = 1e-05
HALF_ROOT = 0.7071067811865476
INV_ROOT_TAU = 0.3989422804014327
F32 = jnp.float32
BF16 = jnp.bfloat16

ROLE = ((6, 4, 0, 3), (7, 1, 2, 5))


def normalize(values):
    center = values - jnp.mean(values, axis=-1, keepdims=True)
    inv_scale = lax.rsqrt(jnp.mean(center * center, axis=-1, keepdims=True) + EPS)
    return (center * inv_scale, inv_scale)


def norm_back(grad_norm, normed, inv_scale):
    mean_grad = jnp.mean(grad_norm, axis=-1, keepdims=True)
    mean_proj = jnp.mean(grad_norm * normed, axis=-1, keepdims=True)
    return inv_scale * (grad_norm - mean_grad - normed * mean_proj)


def gelu_parts(pre_act):
    cumul = 0.5 * (1.0 + lax.erf(pre_act * HALF_ROOT))
    density = jnp.exp(-0.5 * pre_act * pre_act) * INV_ROOT_TAU
    return (pre_act * cumul, cumul + pre_act * density)


def contract_rows(left, right):
    return lax.dot_general(left, right, (((0,), (0,)), ((), ())), preferred_element_type=F32)


def contract_cols(left, right):
    return lax.dot_general(left, right, (((1,), (1,)), ((), ())), preferred_element_type=F32)


def copy_role(stage, outs, axis, role, first, count, sem):
    start = (axis * 8 + role) * SIDE + first
    target = outs[axis * SIDE + role // 2].at[pl.ds(role % 2 * SIDE + first, count)]
    return pltpu.make_async_copy(stage.at[pl.ds(start, count)], target, sem)


def forward_kernel(dest, mix, out_grad, w_up, w_down, gain_first, gain_second, *refs):
    hidden, slope, grad_wide, grad_mid = refs[:4]
    outs, (active, stage, sems) = refs[4:12], refs[12:]
    step = pl.program_id(0)

    @pl.when(step == 0)
    def _():
        normed, _ = normalize(mix[...].astype(F32))
        hidden[...] = (normed * gain_first[...]).astype(BF16)

    @pl.when(step < SIDE)
    def _():
        pre_act = jnp.dot(hidden[...], w_up[...], preferred_element_type=F32)
        act_value, act_slope = gelu_parts(pre_act)
        act_value = act_value.astype(BF16)
        active[step] = act_value
        slope[0] = act_slope
        part = jnp.dot(act_value, w_down[...], preferred_element_type=F32)

        @pl.when(step == 0)
        def _():
            grad_wide[...] = part + hidden[...].astype(F32)

        @pl.when(step > 0)
        def _():
            grad_wide[...] += part

    @pl.when(step == SIDE - 1)
    def _():
        normed_out, inv_out = normalize(grad_wide[...])
        wide = norm_back(out_grad[...].astype(F32) * gain_second[...], normed_out, inv_out)
        grad_wide[...] = wide
        grad_mid[...] = wide.astype(BF16)

    def copies(s):
        whole_lines = [
            copy_role(stage, outs, 1, ROLE[half][s], 0, SIDE, sems.at[s, 8 + half])
            for half in range(2)
        ]
        return whole_lines + [
            copy_role(stage, outs, 0, role, s, 1, sems.at[s, role]) for role in range(8)
        ]

    @pl.when(step >= SIDE)
    def _():
        line = lax.rem(dest[4 * SIDE * SIDE] + step - SIDE, SIDE)
        part = contract_rows(active[line], grad_mid[...]).astype(BF16)
        for k in range(16):
            stage[dest[line * 16 + k]] = part[k * BLOCK : (k + 1) * BLOCK]

    for s in range(SIDE):

        @pl.when(step == SIDE + s)
        def _():
            for copy in copies(s):
                copy.start()

    @pl.when(step == 2 * SIDE - 1)
    def _():
        for s in range(SIDE):
            for copy in copies(s):
                copy.wait()


def backward_kernel(
    dest, mix, hidden, slope, grad_wide, grad_mid, w_up, w_down, gain_first, *refs
):
    grad_sum, outs = refs[0], refs[1:9]
    turned, grad_hidden, stage, sems = refs[9:]
    step = pl.program_id(0)

    def copies(part):
        axis, half = part // 2, part % 2
        return [
            copy_role(stage, outs, axis, ROLE[half][d], 0, SIDE, sems.at[part, d])
            for d in range(SIDE)
        ]

    @pl.when(step == 0)
    def _():
        turned[...] = hidden[...].T

    grad_act = contract_cols(grad_mid[...], w_down[...])
    grad_pre = (grad_act * slope[0]).astype(BF16)
    part = jnp.dot(turned[...], grad_pre, preferred_element_type=F32).astype(BF16)
    for k in range(16):
        stage[dest[k * 4 + step]] = part[k * BLOCK : (k + 1) * BLOCK]
    for q in range(SIDE):

        @pl.when(step == q)
        def _():
            for copy in copies(q):
                copy.start()

    part = contract_cols(grad_pre, w_up[...])

    @pl.when(step == 0)
    def _():
        grad_hidden[...] = part + grad_wide[...]

    @pl.when(step > 0)
    def _():
        grad_hidden[...] += part

    @pl.when(step == SIDE - 1)
    def _():
        normed, inv_scale = normalize(mix[...].astype(F32))
        total = norm_back(grad_hidden[...] * gain_first[...], normed, inv_scale)
        grad_sum[...] = total.T.astype(BF16)
        for q in range(SIDE):
            for copy in copies(q):
                copy.wait()


def seat_kernel(grad_sum, swapped, owner, slot, sent):
    owners, rows = sent.shape[0], owner.shape[1]
    width = sent.shape[2]
    iota = functools.partial(lax.broadcasted_iota, jnp.int32)
    embed = (grad_sum[...].astype(F32) + swapped[...].astype(F32)).astype(BF16)
    owner_hot = iota((owners, rows), 0) == owner[...]
    earlier = (iota((rows, rows), 0) < iota((rows, rows), 1)).astype(F32).astype(BF16)
    ahead = jnp.dot(
        owner_hot.astype(F32).astype(BF16), earlier, preferred_element_type=F32
    )
    rank = jnp.sum(jnp.where(owner_hot, ahead, 0.0), axis=0, keepdims=True).astype(jnp.int32)
    rank_hot = (iota((width, rows), 0) == rank).astype(F32).astype(BF16)
    slot_next = jnp.where(owner_hot, (slot[...] + 1).astype(F32), 0.0).astype(BF16)
    slots = contract_cols(slot_next, rank_hot)
    seat = owner[...] * SEAT + rank
    picker = (iota((owners * SEAT, rows), 0) == seat).astype(F32).astype(BF16)
    chosen = contract_cols(picker, embed).reshape(owners, SEAT, width)
    at_cap = iota((1, SEAT, 1), 1) == CAP
    sent[...] = jnp.where(at_cap, slots[:, None, :], chosen).astype(BF16)


def add(*refs):
    total = refs[0].astype(F32)
    for ref in refs[1:]:
        total = total + ref.astype(F32)
    return total


def first_kernel(*refs):
    ins, outs = refs[:-4], refs[-4:]
    for axis in range(2):
        for mat in range(2):
            keep, up, down = ins[(axis * 2 + mat) * 3 : (axis * 2 + mat) * 3 + 3]
            rows = pl.ds(mat * SIDE, SIDE)
            outs[axis * 2][rows] = add(keep[:SIDE], up[...]).astype(BF16)
            outs[axis * 2 + 1][rows] = add(keep[SIDE:], down[...]).astype(BF16)


def second_kernel(*refs):
    ins, outs = refs[:-8], refs[-8:]
    for axis in range(2):
        here = ins[axis * 8 : axis * 8 + 8]
        for mat in range(2):
            keep, up, down = here[mat * 3 : mat * 3 + 3]
            rows = slice(mat * SIDE, (mat + 1) * SIDE)
            low = add(keep[:SIDE], down[...], here[6][rows])
            high = add(keep[SIDE:], up[...], here[7][rows])
            for half, total in enumerate((low, high)):
                for away in range(SIDE):
                    out = outs[axis * SIDE + away]
                    out[2 * mat + half] = total[away].astype(out.dtype)


def last_kernel(*refs):
    ins, (grad_up, grad_down) = refs[:-2], refs[-2:]
    width = grad_down.shape[1]
    for axis in range(2):
        for half in range(2):
            part = 2 * axis + half
            here = ins[axis * SIDE : (axis + 1) * SIDE]
            grad_down[part * BLOCK : (part + 1) * BLOCK, :] = add(*(ref[half] for ref in here))
            grad_up[:, part * width : (part + 1) * width] = add(*(ref[2 + half] for ref in here))


def moves(axis, sign):
    pairs = []
    for index in range(SIDE * SIDE):
        y, x = divmod(index, SIDE)
        if axis == 0:
            x = (x + sign) % SIDE
        else:
            y = (y + sign) % SIDE
        pairs.append((index, y * SIDE + x))
    return pairs


def shift(value, axis, sign):
    return lax.ppermute(value, "dp", moves(axis, sign))


def block_places():
    me = lax.axis_index("dp")
    flat = jnp.arange(SIDE * SIDE * 4, dtype=jnp.int32)
    owner, part = flat // 4, flat % 4
    away_x = (owner % SIDE - me % SIDE) % SIDE
    away_y = (owner // SIDE - me // SIDE) % SIDE
    axis, half = part // 2, part % 2
    first = jnp.where(axis == 0, away_x, away_y)
    inner = jnp.where(axis == 0, away_y, away_x)
    role = jnp.zeros_like(flat)
    for h in range(2):
        for d in range(SIDE):
            role = jnp.where((half == h) & (first == d), ROLE[h][d], role)
    places = (axis * 8 + role) * SIDE + inner
    return jnp.concatenate([places, jnp.full((SIDE,), me // SIDE, jnp.int32)])


def params(*semantics, limit=60):
    return pltpu.CompilerParams(
        dimension_semantics=semantics or None, vmem_limit_bytes=limit * 1024 * 1024
    )


def cost(flops, size):
    return pl.CostEstimate(flops=flops, bytes_accessed=size, transcendentals=0)


def whole(shape):
    return pl.BlockSpec(shape, lambda *_: (0,) * len(shape))


ANY = pl.BlockSpec(memory_space=pl.ANY)


def per_device(mix_input, out_grad, w_up, w_down, gain_first, gain_second, owner_dev, slot_row):
    rows, _, width = mix_input.shape
    hidden_units = w_up.shape[2]
    chunk = hidden_units // SIDE
    owners = lax.axis_size("dp")
    pieces = lax.axis_size("token")
    mix, out_g = mix_input.reshape(rows, width), out_grad.reshape(rows, width)
    up_mat, down_mat = w_up[0], w_down[0]
    dest = block_places()
    group = jax.ShapeDtypeStruct((8, BLOCK, width), BF16)
    tall = whole((rows, width))
    gain = whole((1, width))
    clamp = lambda i: jnp.minimum(i, SIDE - 1)
    stage = [pltpu.VMEM((64, BLOCK, width), BF16), pltpu.SemaphoreType.DMA((SIDE, 10))]
    matmul = 2 * rows * width * hidden_units
    hidden, slope, grad_wide, grad_mid, *down_parts = pl.pallas_call(
        forward_kernel,
        grid_spec=pltpu.PrefetchScalarGridSpec(
            num_scalar_prefetch=1,
            grid=(2 * SIDE,),
            in_specs=[
                tall,
                tall,
                pl.BlockSpec((width, chunk), lambda i, _: (0, clamp(i))),
                pl.BlockSpec((chunk, width), lambda i, _: (clamp(i), 0)),
                gain,
                gain,
            ],
            out_specs=[
                tall,
                pl.BlockSpec((1, rows, chunk), lambda i, _: (clamp(i), 0, 0)),
                tall,
                tall,
            ]
            + [ANY] * 8,
            scratch_shapes=[pltpu.VMEM((SIDE, rows, chunk), BF16)] + stage,
        ),
        out_shape=[
            jax.ShapeDtypeStruct((rows, width), BF16),
            jax.ShapeDtypeStruct((SIDE, rows, chunk), F32),
            jax.ShapeDtypeStruct((rows, width), F32),
            jax.ShapeDtypeStruct((rows, width), BF16),
        ]
        + [group] * 8,
        compiler_params=params("arbitrary"),
        cost_estimate=cost(3 * matmul, 25_000_000),
        name="forward_and_grad_down",
    )(dest, mix, out_g, up_mat, down_mat, gain_first, gain_second)

    def send(parts):
        return [(shift(parts[4 * a], a, 1), shift(parts[4 * a + 1], a, -1)) for a in range(2)]

    down_got = send(down_parts)

    grad_sum, *up_parts = pl.pallas_call(
        backward_kernel,
        grid_spec=pltpu.PrefetchScalarGridSpec(
            num_scalar_prefetch=1,
            grid=(SIDE,),
            in_specs=[
                tall,
                tall,
                pl.BlockSpec((1, rows, chunk), lambda i, _: (i, 0, 0)),
                tall,
                tall,
                pl.BlockSpec((width, chunk), lambda i, _: (0, i)),
                pl.BlockSpec((chunk, width), lambda i, _: (i, 0)),
                gain,
            ],
            out_specs=[whole((width, rows))] + [ANY] * 8,
            scratch_shapes=[pltpu.VMEM((width, rows), BF16), pltpu.VMEM((rows, width), F32)]
            + stage,
        ),
        out_shape=[jax.ShapeDtypeStruct((width, rows), BF16)] + [group] * 8,
        compiler_params=params("arbitrary"),
        cost_estimate=cost(3 * matmul, 25_000_000),
        name="backward_and_grad_up",
    )(dest, mix, hidden, slope, grad_wide, grad_mid, up_mat, down_mat, gain_first)

    leaving = [up_parts[k] for k in (0, 1, 4, 5)]
    leaving, grad_sum, down_got = lax.optimization_barrier((leaving, grad_sum, down_got))
    up_parts = [*leaving[:2], *up_parts[2:4], *leaving[2:], *up_parts[6:]]
    up_got = send(up_parts)

    swapped = lax.all_to_all(
        grad_sum.reshape(pieces, width // pieces, rows),
        "token",
        split_axis=0,
        concat_axis=0,
        tiled=True,
    ).reshape(width, rows)

    mats = ((down_parts, down_got), (up_parts, up_got))

    def lines(count, part=0):
        return pl.BlockSpec((count, ROWS, width), lambda i: (part, i, 0))

    def combine(kernel, specs, args, counts, dtypes, name):
        return pl.pallas_call(
            kernel,
            grid=(BLOCK // ROWS,),
            in_specs=specs,
            out_specs=[lines(n) for n in counts],
            out_shape=[
                jax.ShapeDtypeStruct((n, BLOCK, width), t) for n, t in zip(counts, dtypes)
            ],
            compiler_params=params("arbitrary"),
            cost_estimate=cost(1_000_000, 7_000_000),
            name=name,
        )(*args)

    args, specs = [], []
    for a in range(2):
        for parts, got in mats:
            args += [parts[4 * a + 2], *got[a]]
            specs += [lines(8), lines(4), lines(4)]
    both = combine(first_kernel, specs, args, [8] * 4, [BF16] * 4, "first_sums")
    both_got = [shift(both[2 * a + s], a, 1 - 2 * s) for a in range(2) for s in range(2)]

    swapped, _ = lax.optimization_barrier((swapped, both))
    sent = pl.pallas_call(
        seat_kernel,
        out_shape=jax.ShapeDtypeStruct((owners, SEAT, width), BF16),
        compiler_params=params(),
        cost_estimate=cost(2 * owners * SEAT * rows * width, 4_000_000),
    )(grad_sum, swapped, owner_dev.reshape(1, rows), slot_row)
    sent, both_got = lax.optimization_barrier((sent, both_got))

    args, specs = [], []
    for a in range(2):
        for parts, got in mats:
            args += [parts[4 * a + 3], *got[a]]
            specs += [lines(8), lines(4, 1), lines(4, 1)]
        args += both_got[2 * a : 2 * a + 2]
        specs += [lines(8), lines(8)]
    summed = combine(
        second_kernel, specs, args, [4] * 8, [F32, BF16, BF16, BF16] * 2, "second_sums"
    )
    lined = [shift(summed[a * SIDE + d], 1 - a, d) for a in range(2) for d in range(1, SIDE)]
    sent, lined[0] = lax.optimization_barrier((sent, lined[0]))
    landed = lax.all_to_all(sent, "dp", split_axis=0, concat_axis=0, tiled=True)
    args = [summed[0], *lined[:3], summed[SIDE], *lined[3:]]
    grad_up, grad_down = pl.pallas_call(
        last_kernel,
        out_shape=[
            jax.ShapeDtypeStruct((BLOCK, hidden_units), F32),
            jax.ShapeDtypeStruct((4 * BLOCK, width), F32),
        ],
        compiler_params=params(),
        cost_estimate=cost(1_000_000, 4_000_000),
        name="last_sums",
    )(*args)

    slots_in = landed[:, CAP, :SEAT].astype(jnp.int32) - 1
    placer = (
        lax.broadcasted_iota(jnp.int32, (HOT, owners, SEAT), 0) == slots_in[None]
    ).astype(BF16)
    row_grad = jnp.dot(
        placer.reshape(HOT, owners * SEAT),
        landed.reshape(owners * SEAT, width),
        preferred_element_type=F32,
    )
    return (grad_up[None], grad_down[None], row_grad[None])


def solution(mesh):
    placed = (
        P("dp", "token", None),
        P("dp", "token", None),
        P("token", None, None),
        P("token", None, None),
        P("token", None),
        P("token", None),
        P("token", "dp", None),
        P("token", "dp"),
    )
    return jax.shard_map(
        per_device,
        mesh=mesh,
        in_specs=placed,
        out_specs=(P("token", "dp", None), P("token", "dp", None), P("token", "dp", None)),
        check_vma=False,
    )
```

```python
import functools

import jax
import jax.numpy as jnp
from jax import lax
from jax.experimental import pallas as pl
from jax.experimental.pallas import tpu as pltpu
from jax.sharding import PartitionSpec as P

HOT = 256
CAP = 56
SEAT = 64
SIDE = 4
BLOCK = 48
ROWS = 48

EPS = 1e-05
HALF_ROOT = 0.7071067811865476
INV_ROOT_TAU = 0.3989422804014327
F32 = jnp.float32
BF16 = jnp.bfloat16

ROLE = ((6, 4, 0, 3), (7, 1, 2, 5))


def normalize(values):
    center = values - jnp.mean(values, axis=-1, keepdims=True)
    inv_scale = lax.rsqrt(jnp.mean(center * center, axis=-1, keepdims=True) + EPS)
    return (center * inv_scale, inv_scale)


def norm_back(grad_norm, normed, inv_scale):
    mean_grad = jnp.mean(grad_norm, axis=-1, keepdims=True)
    mean_proj = jnp.mean(grad_norm * normed, axis=-1, keepdims=True)
    return inv_scale * (grad_norm - mean_grad - normed * mean_proj)


def gelu_parts(pre_act):
    cumul = 0.5 * (1.0 + lax.erf(pre_act * HALF_ROOT))
    density = jnp.exp(-0.5 * pre_act * pre_act) * INV_ROOT_TAU
    return (pre_act * cumul, cumul + pre_act * density)


def contract_rows(left, right):
    return lax.dot_general(left, right, (((0,), (0,)), ((), ())), preferred_element_type=F32)


def contract_cols(left, right):
    return lax.dot_general(left, right, (((1,), (1,)), ((), ())), preferred_element_type=F32)


def copy_role(stage, outs, axis, role, first, count, sem):
    start = (axis * 8 + role) * SIDE + first
    target = outs[axis * SIDE + role // 2].at[pl.ds(role % 2 * SIDE + first, count)]
    return pltpu.make_async_copy(stage.at[pl.ds(start, count)], target, sem)


def forward_kernel(dest, mix, out_grad, w_up, w_down, gain_first, gain_second, *refs):
    hidden, slope, grad_wide, grad_mid = refs[:4]
    outs, (active, stage, sems) = refs[4:12], refs[12:]
    step = pl.program_id(0)

    @pl.when(step == 0)
    def _():
        normed, _ = normalize(mix[...].astype(F32))
        hidden[...] = (normed * gain_first[...]).astype(BF16)

    @pl.when(step < SIDE)
    def _():
        pre_act = jnp.dot(hidden[...], w_up[...], preferred_element_type=F32)
        act_value, act_slope = gelu_parts(pre_act)
        act_value = act_value.astype(BF16)
        active[step] = act_value
        slope[0] = act_slope
        part = jnp.dot(act_value, w_down[...], preferred_element_type=F32)

        @pl.when(step == 0)
        def _():
            grad_wide[...] = part + hidden[...].astype(F32)

        @pl.when(step > 0)
        def _():
            grad_wide[...] += part

    @pl.when(step == SIDE - 1)
    def _():
        normed_out, inv_out = normalize(grad_wide[...])
        wide = norm_back(out_grad[...].astype(F32) * gain_second[...], normed_out, inv_out)
        grad_wide[...] = wide
        grad_mid[...] = wide.astype(BF16)

    def copies(s):
        whole_lines = [
            copy_role(stage, outs, 1, ROLE[half][s], 0, SIDE, sems.at[s, 8 + half])
            for half in range(2)
        ]
        return whole_lines + [
            copy_role(stage, outs, 0, role, s, 1, sems.at[s, role]) for role in range(8)
        ]

    @pl.when(step >= SIDE)
    def _():
        line = lax.rem(dest[4 * SIDE * SIDE] + step - SIDE, SIDE)
        part = contract_rows(active[line], grad_mid[...]).astype(BF16)
        for k in range(16):
            stage[dest[line * 16 + k]] = part[k * BLOCK : (k + 1) * BLOCK]

    for s in range(SIDE):

        @pl.when(step == SIDE + s)
        def _():
            for copy in copies(s):
                copy.start()

    @pl.when(step == 2 * SIDE - 1)
    def _():
        for s in range(SIDE):
            for copy in copies(s):
                copy.wait()


def backward_kernel(
    dest, mix, hidden, slope, grad_wide, grad_mid, w_up, w_down, gain_first, *refs
):
    grad_sum, outs = refs[0], refs[1:9]
    turned, grad_hidden, stage, sems = refs[9:]
    step = pl.program_id(0)

    def copies(part):
        axis, half = part // 2, part % 2
        return [
            copy_role(stage, outs, axis, ROLE[half][d], 0, SIDE, sems.at[part, d])
            for d in range(SIDE)
        ]

    @pl.when(step == 0)
    def _():
        turned[...] = hidden[...].T

    grad_act = contract_cols(grad_mid[...], w_down[...])
    grad_pre = (grad_act * slope[0]).astype(BF16)
    part = jnp.dot(turned[...], grad_pre, preferred_element_type=F32).astype(BF16)
    for k in range(16):
        stage[dest[k * 4 + step]] = part[k * BLOCK : (k + 1) * BLOCK]
    for q in range(SIDE):

        @pl.when(step == q)
        def _():
            for copy in copies(q):
                copy.start()

    part = contract_cols(grad_pre, w_up[...])

    @pl.when(step == 0)
    def _():
        grad_hidden[...] = part + grad_wide[...]

    @pl.when(step > 0)
    def _():
        grad_hidden[...] += part

    @pl.when(step == SIDE - 1)
    def _():
        normed, inv_scale = normalize(mix[...].astype(F32))
        total = norm_back(grad_hidden[...] * gain_first[...], normed, inv_scale)
        grad_sum[...] = total.T.astype(BF16)
        for q in range(SIDE):
            for copy in copies(q):
                copy.wait()


def seat_kernel(grad_sum, swapped, owner, slot, sent):
    owners, rows = sent.shape[0], owner.shape[1]
    width = sent.shape[2]
    iota = functools.partial(lax.broadcasted_iota, jnp.int32)
    embed = (grad_sum[...].astype(F32) + swapped[...].astype(F32)).astype(BF16)
    owner_hot = iota((owners, rows), 0) == owner[...]
    earlier = (iota((rows, rows), 0) < iota((rows, rows), 1)).astype(F32).astype(BF16)
    ahead = jnp.dot(
        owner_hot.astype(F32).astype(BF16), earlier, preferred_element_type=F32
    )
    rank = jnp.sum(jnp.where(owner_hot, ahead, 0.0), axis=0, keepdims=True).astype(jnp.int32)
    rank_hot = (iota((width, rows), 0) == rank).astype(F32).astype(BF16)
    slot_next = jnp.where(owner_hot, (slot[...] + 1).astype(F32), 0.0).astype(BF16)
    slots = contract_cols(slot_next, rank_hot)
    seat = owner[...] * SEAT + rank
    picker = (iota((owners * SEAT, rows), 0) == seat).astype(F32).astype(BF16)
    chosen = contract_cols(picker, embed).reshape(owners, SEAT, width)
    at_cap = iota((1, SEAT, 1), 1) == CAP
    sent[...] = jnp.where(at_cap, slots[:, None, :], chosen).astype(BF16)


def add(*refs):
    total = refs[0].astype(F32)
    for ref in refs[1:]:
        total = total + ref.astype(F32)
    return total


def first_kernel(*refs):
    ins, outs = refs[:-4], refs[-4:]
    for axis in range(2):
        for mat in range(2):
            keep, up, down = ins[(axis * 2 + mat) * 3 : (axis * 2 + mat) * 3 + 3]
            rows = pl.ds(mat * SIDE, SIDE)
            outs[axis * 2][rows] = add(keep[:SIDE], up[...]).astype(BF16)
            outs[axis * 2 + 1][rows] = add(keep[SIDE:], down[...]).astype(BF16)


def second_kernel(*refs):
    ins, outs = refs[:-8], refs[-8:]
    for axis in range(2):
        here = ins[axis * 8 : axis * 8 + 8]
        for mat in range(2):
            keep, up, down = here[mat * 3 : mat * 3 + 3]
            rows = slice(mat * SIDE, (mat + 1) * SIDE)
            low = add(keep[:SIDE], down[...], here[6][rows])
            high = add(keep[SIDE:], up[...], here[7][rows])
            for half, total in enumerate((low, high)):
                for away in range(SIDE):
                    out = outs[axis * SIDE + away]
                    out[2 * mat + half] = total[away].astype(out.dtype)


def last_kernel(*refs):
    ins, (grad_up, grad_down) = refs[:-2], refs[-2:]
    width = grad_down.shape[1]
    for axis in range(2):
        for half in range(2):
            part = 2 * axis + half
            here = ins[axis * SIDE : (axis + 1) * SIDE]
            grad_down[part * BLOCK : (part + 1) * BLOCK, :] = add(*(ref[half] for ref in here))
            grad_up[:, part * width : (part + 1) * width] = add(*(ref[2 + half] for ref in here))


def moves(axis, sign):
    pairs = []
    for index in range(SIDE * SIDE):
        y, x = divmod(index, SIDE)
        if axis == 0:
            x = (x + sign) % SIDE
        else:
            y = (y + sign) % SIDE
        pairs.append((index, y * SIDE + x))
    return pairs


def shift(value, axis, sign):
    return lax.ppermute(value, "dp", moves(axis, sign))


def block_places():
    me = lax.axis_index("dp")
    flat = jnp.arange(SIDE * SIDE * 4, dtype=jnp.int32)
    owner, part = flat // 4, flat % 4
    away_x = (owner % SIDE - me % SIDE) % SIDE
    away_y = (owner // SIDE - me // SIDE) % SIDE
    axis, half = part // 2, part % 2
    first = jnp.where(axis == 0, away_x, away_y)
    inner = jnp.where(axis == 0, away_y, away_x)
    role = jnp.zeros_like(flat)
    for h in range(2):
        for d in range(SIDE):
            role = jnp.where((half == h) & (first == d), ROLE[h][d], role)
    places = (axis * 8 + role) * SIDE + inner
    return jnp.concatenate([places, jnp.full((SIDE,), me // SIDE, jnp.int32)])


def params(*semantics, limit=60):
    return pltpu.CompilerParams(
        dimension_semantics=semantics or None, vmem_limit_bytes=limit * 1024 * 1024
    )


def cost(flops, size):
    return pl.CostEstimate(flops=flops, bytes_accessed=size, transcendentals=0)


def whole(shape):
    return pl.BlockSpec(shape, lambda *_: (0,) * len(shape))


ANY = pl.BlockSpec(memory_space=pl.ANY)


def per_device(mix_input, out_grad, w_up, w_down, gain_first, gain_second, owner_dev, slot_row):
    rows, _, width = mix_input.shape
    hidden_units = w_up.shape[2]
    chunk = hidden_units // SIDE
    owners = lax.axis_size("dp")
    pieces = lax.axis_size("token")
    mix, out_g = mix_input.reshape(rows, width), out_grad.reshape(rows, width)
    up_mat, down_mat = w_up[0], w_down[0]
    dest = block_places()
    group = jax.ShapeDtypeStruct((8, BLOCK, width), BF16)
    tall = whole((rows, width))
    gain = whole((1, width))
    clamp = lambda i: jnp.minimum(i, SIDE - 1)
    stage = [pltpu.VMEM((64, BLOCK, width), BF16), pltpu.SemaphoreType.DMA((SIDE, 10))]
    matmul = 2 * rows * width * hidden_units
    hidden, slope, grad_wide, grad_mid, *down_parts = pl.pallas_call(
        forward_kernel,
        grid_spec=pltpu.PrefetchScalarGridSpec(
            num_scalar_prefetch=1,
            grid=(2 * SIDE,),
            in_specs=[
                tall,
                tall,
                pl.BlockSpec((width, chunk), lambda i, _: (0, clamp(i))),
                pl.BlockSpec((chunk, width), lambda i, _: (clamp(i), 0)),
                gain,
                gain,
            ],
            out_specs=[
                tall,
                pl.BlockSpec((1, rows, chunk), lambda i, _: (clamp(i), 0, 0)),
                tall,
                tall,
            ]
            + [ANY] * 8,
            scratch_shapes=[pltpu.VMEM((SIDE, rows, chunk), BF16)] + stage,
        ),
        out_shape=[
            jax.ShapeDtypeStruct((rows, width), BF16),
            jax.ShapeDtypeStruct((SIDE, rows, chunk), F32),
            jax.ShapeDtypeStruct((rows, width), F32),
            jax.ShapeDtypeStruct((rows, width), BF16),
        ]
        + [group] * 8,
        compiler_params=params("arbitrary"),
        cost_estimate=cost(3 * matmul, 25_000_000),
        name="forward_and_grad_down",
    )(dest, mix, out_g, up_mat, down_mat, gain_first, gain_second)

    def send(parts):
        return [(shift(parts[4 * a], a, 1), shift(parts[4 * a + 1], a, -1)) for a in range(2)]

    down_got = send(down_parts)

    grad_sum, *up_parts = pl.pallas_call(
        backward_kernel,
        grid_spec=pltpu.PrefetchScalarGridSpec(
            num_scalar_prefetch=1,
            grid=(SIDE,),
            in_specs=[
                tall,
                tall,
                pl.BlockSpec((1, rows, chunk), lambda i, _: (i, 0, 0)),
                tall,
                tall,
                pl.BlockSpec((width, chunk), lambda i, _: (0, i)),
                pl.BlockSpec((chunk, width), lambda i, _: (i, 0)),
                gain,
            ],
            out_specs=[whole((width, rows))] + [ANY] * 8,
            scratch_shapes=[pltpu.VMEM((width, rows), BF16), pltpu.VMEM((rows, width), F32)]
            + stage,
        ),
        out_shape=[jax.ShapeDtypeStruct((width, rows), BF16)] + [group] * 8,
        compiler_params=params("arbitrary"),
        cost_estimate=cost(3 * matmul, 25_000_000),
        name="backward_and_grad_up",
    )(dest, mix, hidden, slope, grad_wide, grad_mid, up_mat, down_mat, gain_first)

    leaving = [up_parts[k] for k in (0, 1, 4, 5)]
    leaving, grad_sum, down_got = lax.optimization_barrier((leaving, grad_sum, down_got))
    up_parts = [*leaving[:2], *up_parts[2:4], *leaving[2:], *up_parts[6:]]
    up_got = send(up_parts)

    swapped = lax.all_to_all(
        grad_sum.reshape(pieces, width // pieces, rows),
        "token",
        split_axis=0,
        concat_axis=0,
        tiled=True,
    ).reshape(width, rows)

    mats = ((down_parts, down_got), (up_parts, up_got))

    def lines(count, part=0):
        return pl.BlockSpec((count, ROWS, width), lambda i: (part, i, 0))

    def combine(kernel, specs, args, counts, dtypes, name):
        return pl.pallas_call(
            kernel,
            grid=(BLOCK // ROWS,),
            in_specs=specs,
            out_specs=[lines(n) for n in counts],
            out_shape=[
                jax.ShapeDtypeStruct((n, BLOCK, width), t) for n, t in zip(counts, dtypes)
            ],
            compiler_params=params("arbitrary"),
            cost_estimate=cost(1_000_000, 7_000_000),
            name=name,
        )(*args)

    args, specs = [], []
    for a in range(2):
        for parts, got in mats:
            args += [parts[4 * a + 2], *got[a]]
            specs += [lines(8), lines(4), lines(4)]
    both = combine(first_kernel, specs, args, [8] * 4, [BF16] * 4, "first_sums")
    both_got = [shift(both[2 * a + s], a, 1 - 2 * s) for a in range(2) for s in range(2)]

    swapped, _ = lax.optimization_barrier((swapped, both))
    sent = pl.pallas_call(
        seat_kernel,
        out_shape=jax.ShapeDtypeStruct((owners, SEAT, width), BF16),
        compiler_params=params(),
        cost_estimate=cost(2 * owners * SEAT * rows * width, 4_000_000),
    )(grad_sum, swapped, owner_dev.reshape(1, rows), slot_row)
    sent, both_got = lax.optimization_barrier((sent, both_got))

    args, specs = [], []
    for a in range(2):
        for parts, got in mats:
            args += [parts[4 * a + 3], *got[a]]
            specs += [lines(8), lines(4, 1), lines(4, 1)]
        args += both_got[2 * a : 2 * a + 2]
        specs += [lines(8), lines(8)]
    summed = combine(
        second_kernel, specs, args, [4] * 8, [F32, BF16, BF16, BF16] * 2, "second_sums"
    )
    lined = [shift(summed[a * SIDE + d], 1 - a, d) for a in range(2) for d in range(1, SIDE)]
    sent, lined = lax.optimization_barrier((sent, lined))
    landed = lax.all_to_all(sent, "dp", split_axis=0, concat_axis=0, tiled=True)
    args = [summed[0], *lined[:3], summed[SIDE], *lined[3:]]
    grad_up, grad_down = pl.pallas_call(
        last_kernel,
        out_shape=[
            jax.ShapeDtypeStruct((BLOCK, hidden_units), F32),
            jax.ShapeDtypeStruct((4 * BLOCK, width), F32),
        ],
        compiler_params=params(),
        cost_estimate=cost(1_000_000, 4_000_000),
        name="last_sums",
    )(*args)

    slots_in = landed[:, CAP, :SEAT].astype(jnp.int32) - 1
    placer = (
        lax.broadcasted_iota(jnp.int32, (HOT, owners, SEAT), 0) == slots_in[None]
    ).astype(BF16)
    row_grad = jnp.dot(
        placer.reshape(HOT, owners * SEAT),
        landed.reshape(owners * SEAT, width),
        preferred_element_type=F32,
    )
    return (grad_up[None], grad_down[None], row_grad[None])


def solution(mesh):
    placed = (
        P("dp", "token", None),
        P("dp", "token", None),
        P("token", None, None),
        P("token", None, None),
        P("token", None),
        P("token", None),
        P("token", "dp", None),
        P("token", "dp"),
    )
    return jax.shard_map(
        per_device,
        mesh=mesh,
        in_specs=placed,
        out_specs=(P("token", "dp", None), P("token", "dp", None), P("token", "dp", None)),
        check_vma=False,
    )
```

```python
import functools

import jax
import jax.numpy as jnp
from jax import lax
from jax.experimental import pallas as pl
from jax.experimental.pallas import tpu as pltpu
from jax.sharding import PartitionSpec as P

HOT = 256
CAP = 56
SEAT = 64
SIDE = 4
BLOCK = 48
ROWS = 48

EPS = 1e-05
HALF_ROOT = 0.7071067811865476
INV_ROOT_TAU = 0.3989422804014327
F32 = jnp.float32
BF16 = jnp.bfloat16

ROLE = ((6, 4, 0, 3), (7, 1, 2, 5))


def normalize(values):
    center = values - jnp.mean(values, axis=-1, keepdims=True)
    inv_scale = lax.rsqrt(jnp.mean(center * center, axis=-1, keepdims=True) + EPS)
    return (center * inv_scale, inv_scale)


def norm_back(grad_norm, normed, inv_scale):
    mean_grad = jnp.mean(grad_norm, axis=-1, keepdims=True)
    mean_proj = jnp.mean(grad_norm * normed, axis=-1, keepdims=True)
    return inv_scale * (grad_norm - mean_grad - normed * mean_proj)


def gelu_parts(pre_act):
    cumul = 0.5 * (1.0 + lax.erf(pre_act * HALF_ROOT))
    density = jnp.exp(-0.5 * pre_act * pre_act) * INV_ROOT_TAU
    return (pre_act * cumul, cumul + pre_act * density)


def contract_rows(left, right):
    return lax.dot_general(left, right, (((0,), (0,)), ((), ())), preferred_element_type=F32)


def contract_cols(left, right):
    return lax.dot_general(left, right, (((1,), (1,)), ((), ())), preferred_element_type=F32)


def copy_role(stage, outs, axis, role, first, count, sem):
    start = (axis * 8 + role) * SIDE + first
    target = outs[axis * SIDE + role // 2].at[pl.ds(role % 2 * SIDE + first, count)]
    return pltpu.make_async_copy(stage.at[pl.ds(start, count)], target, sem)


def forward_kernel(dest, mix, out_grad, w_up, w_down, gain_first, gain_second, *refs):
    hidden, slope, grad_wide, grad_mid = refs[:4]
    outs, (active, stage, sems) = refs[4:12], refs[12:]
    step = pl.program_id(0)

    @pl.when(step == 0)
    def _():
        normed, _ = normalize(mix[...].astype(F32))
        hidden[...] = (normed * gain_first[...]).astype(BF16)

    @pl.when(step < SIDE)
    def _():
        pre_act = jnp.dot(hidden[...], w_up[...], preferred_element_type=F32)
        act_value, act_slope = gelu_parts(pre_act)
        act_value = act_value.astype(BF16)
        active[step] = act_value
        slope[0] = act_slope
        part = jnp.dot(act_value, w_down[...], preferred_element_type=F32)

        @pl.when(step == 0)
        def _():
            grad_wide[...] = part + hidden[...].astype(F32)

        @pl.when(step > 0)
        def _():
            grad_wide[...] += part

    @pl.when(step == SIDE - 1)
    def _():
        normed_out, inv_out = normalize(grad_wide[...])
        wide = norm_back(out_grad[...].astype(F32) * gain_second[...], normed_out, inv_out)
        grad_wide[...] = wide
        grad_mid[...] = wide.astype(BF16)

    def copies(s):
        whole_lines = [
            copy_role(stage, outs, 1, ROLE[half][s], 0, SIDE, sems.at[s, 8 + half])
            for half in range(2)
        ]
        return whole_lines + [
            copy_role(stage, outs, 0, role, s, 1, sems.at[s, role]) for role in range(8)
        ]

    @pl.when(step >= SIDE)
    def _():
        line = lax.rem(dest[4 * SIDE * SIDE] + step - SIDE, SIDE)
        part = contract_rows(active[line], grad_mid[...]).astype(BF16)
        for k in range(16):
            stage[dest[line * 16 + k]] = part[k * BLOCK : (k + 1) * BLOCK]

    for s in range(SIDE):

        @pl.when(step == SIDE + s)
        def _():
            for copy in copies(s):
                copy.start()

    @pl.when(step == 2 * SIDE - 1)
    def _():
        for s in range(SIDE):
            for copy in copies(s):
                copy.wait()


def backward_kernel(
    dest, mix, hidden, slope, grad_wide, grad_mid, w_up, w_down, gain_first, *refs
):
    grad_sum, outs = refs[0], refs[1:9]
    turned, grad_hidden, stage, sems = refs[9:]
    step = pl.program_id(0)

    def copies(part):
        axis, half = part // 2, part % 2
        return [
            copy_role(stage, outs, axis, ROLE[half][d], 0, SIDE, sems.at[part, d])
            for d in range(SIDE)
        ]

    @pl.when(step == 0)
    def _():
        turned[...] = hidden[...].T

    grad_act = contract_cols(grad_mid[...], w_down[...])
    grad_pre = (grad_act * slope[0]).astype(BF16)
    part = jnp.dot(turned[...], grad_pre, preferred_element_type=F32).astype(BF16)
    for k in range(16):
        stage[dest[k * 4 + step]] = part[k * BLOCK : (k + 1) * BLOCK]
    for q in range(SIDE):

        @pl.when(step == q)
        def _():
            for copy in copies(q):
                copy.start()

    part = contract_cols(grad_pre, w_up[...])

    @pl.when(step == 0)
    def _():
        grad_hidden[...] = part + grad_wide[...]

    @pl.when(step > 0)
    def _():
        grad_hidden[...] += part

    @pl.when(step == SIDE - 1)
    def _():
        normed, inv_scale = normalize(mix[...].astype(F32))
        total = norm_back(grad_hidden[...] * gain_first[...], normed, inv_scale)
        grad_sum[...] = total.T.astype(BF16)
        for q in range(SIDE):
            for copy in copies(q):
                copy.wait()


def seat_kernel(grad_sum, swapped, owner, slot, sent):
    owners, rows = sent.shape[0], owner.shape[1]
    width = sent.shape[2]
    iota = functools.partial(lax.broadcasted_iota, jnp.int32)
    embed = (grad_sum[...].astype(F32) + swapped[...].astype(F32)).astype(BF16)
    owner_hot = iota((owners, rows), 0) == owner[...]
    earlier = (iota((rows, rows), 0) < iota((rows, rows), 1)).astype(F32).astype(BF16)
    ahead = jnp.dot(
        owner_hot.astype(F32).astype(BF16), earlier, preferred_element_type=F32
    )
    rank = jnp.sum(jnp.where(owner_hot, ahead, 0.0), axis=0, keepdims=True).astype(jnp.int32)
    rank_hot = (iota((width, rows), 0) == rank).astype(F32).astype(BF16)
    slot_next = jnp.where(owner_hot, (slot[...] + 1).astype(F32), 0.0).astype(BF16)
    slots = contract_cols(slot_next, rank_hot)
    seat = owner[...] * SEAT + rank
    picker = (iota((owners * SEAT, rows), 0) == seat).astype(F32).astype(BF16)
    chosen = contract_cols(picker, embed).reshape(owners, SEAT, width)
    at_cap = iota((1, SEAT, 1), 1) == CAP
    sent[...] = jnp.where(at_cap, slots[:, None, :], chosen).astype(BF16)


def add(*refs):
    total = refs[0].astype(F32)
    for ref in refs[1:]:
        total = total + ref.astype(F32)
    return total


def first_kernel(*refs):
    ins, outs = refs[:-4], refs[-4:]
    for axis in range(2):
        for mat in range(2):
            keep, up, down = ins[(axis * 2 + mat) * 3 : (axis * 2 + mat) * 3 + 3]
            rows = pl.ds(mat * SIDE, SIDE)
            outs[axis * 2][rows] = add(keep[:SIDE], up[...]).astype(BF16)
            outs[axis * 2 + 1][rows] = add(keep[SIDE:], down[...]).astype(BF16)


def second_kernel(*refs):
    ins, outs = refs[:-8], refs[-8:]
    for axis in range(2):
        here = ins[axis * 8 : axis * 8 + 8]
        for mat in range(2):
            keep, up, down = here[mat * 3 : mat * 3 + 3]
            rows = slice(mat * SIDE, (mat + 1) * SIDE)
            low = add(keep[:SIDE], down[...], here[6][rows])
            high = add(keep[SIDE:], up[...], here[7][rows])
            for half, total in enumerate((low, high)):
                for away in range(SIDE):
                    out = outs[axis * SIDE + away]
                    out[2 * mat + half] = total[away].astype(out.dtype)


def last_kernel(*refs):
    ins, (grad_up, grad_down) = refs[:-2], refs[-2:]
    width = grad_down.shape[1]
    for axis in range(2):
        for half in range(2):
            part = 2 * axis + half
            here = ins[axis * SIDE : (axis + 1) * SIDE]
            grad_down[part * BLOCK : (part + 1) * BLOCK, :] = add(*(ref[half] for ref in here))
            grad_up[:, part * width : (part + 1) * width] = add(*(ref[2 + half] for ref in here))


def moves(axis, sign):
    pairs = []
    for index in range(SIDE * SIDE):
        y, x = divmod(index, SIDE)
        if axis == 0:
            x = (x + sign) % SIDE
        else:
            y = (y + sign) % SIDE
        pairs.append((index, y * SIDE + x))
    return pairs


def shift(value, axis, sign):
    return lax.ppermute(value, "dp", moves(axis, sign))


def block_places():
    me = lax.axis_index("dp")
    flat = jnp.arange(SIDE * SIDE * 4, dtype=jnp.int32)
    owner, part = flat // 4, flat % 4
    away_x = (owner % SIDE - me % SIDE) % SIDE
    away_y = (owner // SIDE - me // SIDE) % SIDE
    axis, half = part // 2, part % 2
    first = jnp.where(axis == 0, away_x, away_y)
    inner = jnp.where(axis == 0, away_y, away_x)
    role = jnp.zeros_like(flat)
    for h in range(2):
        for d in range(SIDE):
            role = jnp.where((half == h) & (first == d), ROLE[h][d], role)
    places = (axis * 8 + role) * SIDE + inner
    return jnp.concatenate([places, jnp.full((SIDE,), me // SIDE, jnp.int32)])


def params(*semantics, limit=60):
    return pltpu.CompilerParams(
        dimension_semantics=semantics or None, vmem_limit_bytes=limit * 1024 * 1024
    )


def cost(flops, size):
    return pl.CostEstimate(flops=flops, bytes_accessed=size, transcendentals=0)


def whole(shape):
    return pl.BlockSpec(shape, lambda *_: (0,) * len(shape))


ANY = pl.BlockSpec(memory_space=pl.ANY)


def per_device(mix_input, out_grad, w_up, w_down, gain_first, gain_second, owner_dev, slot_row):
    rows, _, width = mix_input.shape
    hidden_units = w_up.shape[2]
    chunk = hidden_units // SIDE
    owners = lax.axis_size("dp")
    pieces = lax.axis_size("token")
    mix, out_g = mix_input.reshape(rows, width), out_grad.reshape(rows, width)
    up_mat, down_mat = w_up[0], w_down[0]
    dest = block_places()
    group = jax.ShapeDtypeStruct((8, BLOCK, width), BF16)
    tall = whole((rows, width))
    gain = whole((1, width))
    clamp = lambda i: jnp.minimum(i, SIDE - 1)
    stage = [pltpu.VMEM((64, BLOCK, width), BF16), pltpu.SemaphoreType.DMA((SIDE, 10))]
    matmul = 2 * rows * width * hidden_units
    hidden, slope, grad_wide, grad_mid, *down_parts = pl.pallas_call(
        forward_kernel,
        grid_spec=pltpu.PrefetchScalarGridSpec(
            num_scalar_prefetch=1,
            grid=(2 * SIDE,),
            in_specs=[
                tall,
                tall,
                pl.BlockSpec((width, chunk), lambda i, _: (0, clamp(i))),
                pl.BlockSpec((chunk, width), lambda i, _: (clamp(i), 0)),
                gain,
                gain,
            ],
            out_specs=[
                tall,
                pl.BlockSpec((1, rows, chunk), lambda i, _: (clamp(i), 0, 0)),
                tall,
                tall,
            ]
            + [ANY] * 8,
            scratch_shapes=[pltpu.VMEM((SIDE, rows, chunk), BF16)] + stage,
        ),
        out_shape=[
            jax.ShapeDtypeStruct((rows, width), BF16),
            jax.ShapeDtypeStruct((SIDE, rows, chunk), F32),
            jax.ShapeDtypeStruct((rows, width), F32),
            jax.ShapeDtypeStruct((rows, width), BF16),
        ]
        + [group] * 8,
        compiler_params=params("arbitrary"),
        cost_estimate=cost(3 * matmul, 25_000_000),
        name="forward_and_grad_down",
    )(dest, mix, out_g, up_mat, down_mat, gain_first, gain_second)

    def send(parts):
        return [(shift(parts[4 * a], a, 1), shift(parts[4 * a + 1], a, -1)) for a in range(2)]

    down_got = send(down_parts)

    grad_sum, *up_parts = pl.pallas_call(
        backward_kernel,
        grid_spec=pltpu.PrefetchScalarGridSpec(
            num_scalar_prefetch=1,
            grid=(SIDE,),
            in_specs=[
                tall,
                tall,
                pl.BlockSpec((1, rows, chunk), lambda i, _: (i, 0, 0)),
                tall,
                tall,
                pl.BlockSpec((width, chunk), lambda i, _: (0, i)),
                pl.BlockSpec((chunk, width), lambda i, _: (i, 0)),
                gain,
            ],
            out_specs=[whole((width, rows))] + [ANY] * 8,
            scratch_shapes=[pltpu.VMEM((width, rows), BF16), pltpu.VMEM((rows, width), F32)]
            + stage,
        ),
        out_shape=[jax.ShapeDtypeStruct((width, rows), BF16)] + [group] * 8,
        compiler_params=params("arbitrary"),
        cost_estimate=cost(3 * matmul, 25_000_000),
        name="backward_and_grad_up",
    )(dest, mix, hidden, slope, grad_wide, grad_mid, up_mat, down_mat, gain_first)

    leaving = [up_parts[k] for k in (0, 1, 4, 5)]
    leaving, grad_sum, down_got = lax.optimization_barrier((leaving, grad_sum, down_got))
    up_parts = [*leaving[:2], *up_parts[2:4], *leaving[2:], *up_parts[6:]]
    up_got = send(up_parts)

    swapped = lax.all_to_all(
        grad_sum.reshape(pieces, width // pieces, rows),
        "token",
        split_axis=0,
        concat_axis=0,
        tiled=True,
    ).reshape(width, rows)

    mats = ((down_parts, down_got), (up_parts, up_got))

    def lines(count, part=0):
        return pl.BlockSpec((count, ROWS, width), lambda i: (part, i, 0))

    def combine(kernel, specs, args, counts, dtypes, name):
        return pl.pallas_call(
            kernel,
            grid=(BLOCK // ROWS,),
            in_specs=specs,
            out_specs=[lines(n) for n in counts],
            out_shape=[
                jax.ShapeDtypeStruct((n, BLOCK, width), t) for n, t in zip(counts, dtypes)
            ],
            compiler_params=params("arbitrary"),
            cost_estimate=cost(1_000_000, 7_000_000),
            name=name,
        )(*args)

    args, specs = [], []
    for a in range(2):
        for parts, got in mats:
            args += [parts[4 * a + 2], *got[a]]
            specs += [lines(8), lines(4), lines(4)]
    both = combine(first_kernel, specs, args, [8] * 4, [BF16] * 4, "first_sums")
    both_got = [shift(both[2 * a + s], a, 1 - 2 * s) for a in range(2) for s in range(2)]

    swapped, _ = lax.optimization_barrier((swapped, both))
    sent = pl.pallas_call(
        seat_kernel,
        out_shape=jax.ShapeDtypeStruct((owners, SEAT, width), BF16),
        compiler_params=params(),
        cost_estimate=cost(2 * owners * SEAT * rows * width, 4_000_000),
    )(grad_sum, swapped, owner_dev.reshape(1, rows), slot_row)
    sent, both_got = lax.optimization_barrier((sent, both_got))
    landed = lax.all_to_all(sent, "dp", split_axis=0, concat_axis=0, tiled=True)

    args, specs = [], []
    for a in range(2):
        for parts, got in mats:
            args += [parts[4 * a + 3], *got[a]]
            specs += [lines(8), lines(4, 1), lines(4, 1)]
        args += both_got[2 * a : 2 * a + 2]
        specs += [lines(8), lines(8)]
    summed = combine(
        second_kernel, specs, args, [4] * 8, [F32, BF16, BF16, BF16] * 2, "second_sums"
    )
    args = []
    for a in range(2):
        args += [summed[a * SIDE]]
        args += [shift(summed[a * SIDE + away], 1 - a, away) for away in range(1, SIDE)]
    grad_up, grad_down = pl.pallas_call(
        last_kernel,
        out_shape=[
            jax.ShapeDtypeStruct((BLOCK, hidden_units), F32),
            jax.ShapeDtypeStruct((4 * BLOCK, width), F32),
        ],
        compiler_params=params(),
        cost_estimate=cost(1_000_000, 4_000_000),
        name="last_sums",
    )(*args)

    slots_in = landed[:, CAP, :SEAT].astype(jnp.int32) - 1
    placer = (
        lax.broadcasted_iota(jnp.int32, (HOT, owners, SEAT), 0) == slots_in[None]
    ).astype(BF16)
    row_grad = jnp.dot(
        placer.reshape(HOT, owners * SEAT),
        landed.reshape(owners * SEAT, width),
        preferred_element_type=F32,
    )
    return (grad_up[None], grad_down[None], row_grad[None])


def solution(mesh):
    placed = (
        P("dp", "token", None),
        P("dp", "token", None),
        P("token", None, None),
        P("token", None, None),
        P("token", None),
        P("token", None),
        P("token", "dp", None),
        P("token", "dp"),
    )
    return jax.shard_map(
        per_device,
        mesh=mesh,
        in_specs=placed,
        out_specs=(P("token", "dp", None), P("token", "dp", None), P("token", "dp", None)),
        check_vma=False,
    )
```
